512 devices in a mesh: seq: 64 (over z_hi, x, y), sub: 8 (over z_lo, core).
Axes of the slice: x: 4, y: 4, z: 16 (z_hi: 4, z_lo: 4; z = z_hi * 4 + z_lo), core: 2. Of those that a mesh axis runs over, the one named last changes fastest.
Arguments:
- queries: bfloat16 [32768, 2048], P('seq', 'sub'), may hold values from -6 to 6, as said below
- keys: bfloat16 [32768, 2048], P('seq', 'sub'), may hold values from -6 to 6
- values: bfloat16 [32768, 2048], P('seq', 'sub'), may hold values from -6 to 6
- offsets: int32 [32768], P('seq'), may hold values from 1 to 64
- negatives: int32 [32768, 15], P('seq'), may hold values from 0 to 511
Outputs:
- grad_queries: bfloat16 [32768, 2048], P('seq', 'sub')
- grad_keys: bfloat16 [32768, 2048], P('seq', 'sub')
- grad_values: bfloat16 [32768, 2048], P('seq', 'sub')
- loss: float32 [], replicated
The draws below stay inside these ranges and needn't reach their ends.
Inputs may be any that keep to these rules, and one draw needn't show every extreme that they name: `queries`: some rows may be closely aligned with the keys they see, giving scores of several hundred. `offsets`: the positive sample of step t is step (t + value) mod 32768.
All inputs are finite; a program needn't handle non-finite values.
Results may differ from the reference program's by a relative error of at most 0.029.
Values may be sent and summed in bfloat16 or wider, within the bound.
A program may use at most 64 MiB of HBM per device.

```python
import math
import jax
import jax.numpy as jnp
from jax import lax

HEADS = 16
DH = 128
D = 2048
ROWS = 512
BLOCK = 512
STRIDE = 64
OFFMAX = 64
K_NEG = 15
TOKENS = 32768


def draw_queries(key, part):
    key = jax.random.fold_in(key, 5)
    return jnp.clip(jax.random.normal(key, (TOKENS, D), jnp.float32), -6.0, 6.0).astype(jnp.bfloat16)


def draw_keys(key, part):
    key = jax.random.fold_in(key, 3)
    return jnp.clip(jax.random.normal(key, (TOKENS, D), jnp.float32), -6.0, 6.0).astype(jnp.bfloat16)


def with_ends(values, stream_key, smallest, high):
    shape = values.shape
    index_at = [jax.random.randint(jax.random.fold_in(stream_key, axis), (), 0, shape[axis]) for axis in range(len(shape))]
    values = values.at[tuple(index_at)].set(smallest)
    longest = shape.index(max(shape))
    index_at[longest] = (index_at[longest] + 1) % shape[longest]
    return values.at[tuple(index_at)].set(high)


def block_scale(own_key, dims, split, low, largest):
    def one(position, blocks):
        steps = jax.random.uniform(jax.random.fold_in(jax.random.fold_in(own_key, 6), position), (blocks,), jnp.float32, low / len(split), largest / len(split))
        return jnp.repeat(jnp.exp(steps), dims[position] // blocks).reshape((-1,) + (1,) * (len(dims) - position - 1))

    loudness = one(*split[0])
    for cut in split[1:]:
        loudness = loudness * one(*cut)
    return loudness


def scatter_about(key, shape, scale, most, cuts=(), held_as=jnp.bfloat16):
    drawn = scale * jax.random.normal(key, shape, jnp.float32)
    if cuts:
        drawn = drawn * block_scale(key, shape, cuts, -0.22, 0.18)
    return jnp.clip(drawn, -most, most).astype(held_as)


def setup_inputs(seed: int = 0) -> dict:
    seeds = jax.random.split(jax.random.key(seed), 6)
    queries = draw_queries(jax.random.fold_in(seeds[5], 71), 0)
    keys = draw_keys(jax.random.fold_in(seeds[5], 71), 0)
    values = scatter_about(seeds[2], (TOKENS, D), 1.0, 6.0, ((0, 64), (1, 8)))
    offsets = with_ends(jax.random.randint(seeds[3], (TOKENS,), 1, OFFMAX + 1), jax.random.fold_in(seeds[3], 1), 1, OFFMAX).astype(jnp.int32)
    negatives = with_ends(jax.random.randint(seeds[4], (TOKENS, K_NEG), 0, ROWS), jax.random.fold_in(seeds[4], 1), 0, ROWS - 1).astype(jnp.int32)
    return dict(queries=queries, keys=keys, values=values, offsets=offsets, negatives=negatives)


EPSILON = 1e-05
TEMPER = 0.1
MASKED = -1e+30

def widen(stored):
    return lax.optimization_barrier(stored).astype(jnp.float32)

def block_probs(query_blk, keys_all, allowed, scaling):
    scores = jnp.einsum('qhe,khe->hqk', query_blk.astype(jnp.float32), keys_all.astype(jnp.float32)) * scaling
    highest = lax.optimization_barrier(jnp.max(jnp.where(allowed, scores, MASKED), axis=2, keepdims=True))
    summed = lax.optimization_barrier(jnp.sum(jnp.where(allowed, jnp.exp(scores - highest), 0.0), axis=2, keepdims=True))
    log_total = highest + jnp.log(summed)
    return jnp.where(allowed, jnp.exp(scores - log_total), 0.0).astype(jnp.bfloat16)

def contrast(positive, negative, squares, target, picked, weight, extended):
    row_count = positive.shape[0]
    radius = jnp.sqrt(squares / D + EPSILON)
    own_radius = radius[:row_count]
    first_factor = 1.0 / (D * TEMPER * own_radius * radius[target])
    rest_factor = 1.0 / (D * TEMPER * own_radius[:, None] * radius[picked])
    first_logit = positive * first_factor
    rest_logit = negative * rest_factor
    logits = jnp.concatenate([first_logit[:, None], rest_logit], axis=1)
    expsum = lax.optimization_barrier(jnp.sum(jnp.exp(logits), axis=1))
    loss_part = jnp.sum(weight * (jnp.log(expsum) - first_logit))
    chosen_mark = (jnp.arange(logits.shape[1], dtype=jnp.int32) == 0).astype(jnp.float32)
    grad_logit = (jnp.exp(logits) / expsum[:, None] - chosen_mark[None, :]) * weight[:, None]
    grad_first = grad_logit[:, 0] * first_factor
    grad_rest = grad_logit[:, 1:] * rest_factor
    wide_rows = widen(extended)
    own_rows = wide_rows[:row_count]
    pulled = grad_first[:, None] * wide_rows[target]
    pushed = jnp.zeros(wide_rows.shape, jnp.float32).at[target].add(grad_first[:, None] * own_rows)
    for column in range(picked.shape[1]):
        chosen_rows = picked[:, column]
        pulled = pulled + grad_rest[:, column:column + 1] * own_rows[chosen_rows]
        pushed = pushed.at[chosen_rows].add(grad_rest[:, column:column + 1] * own_rows)
    grad_ext = pushed.at[:row_count].add(pulled)
    grad_radius = jnp.zeros((wide_rows.shape[0],), jnp.float32)
    grad_radius = grad_radius.at[:row_count].add(-lax.optimization_barrier(jnp.sum(grad_logit * logits, axis=1)) / own_radius)
    grad_radius = grad_radius.at[target].add(-grad_logit[:, 0] * first_logit / radius[target])
    grad_radius = grad_radius.at[picked].add(-grad_logit[:, 1:] * rest_logit / radius[picked])
    return (loss_part, grad_ext, grad_radius)

def reference(queries, keys, values, offsets, negatives):
    panel_count = TOKENS // STRIDE
    scaling = 1.0 / math.sqrt(DH)
    panel_k = keys[STRIDE - 1::STRIDE].reshape(panel_count, HEADS, DH)
    panel_v = values[STRIDE - 1::STRIDE].reshape(panel_count, HEADS, DH)
    panel_pos = jnp.arange(panel_count, dtype=jnp.int32) * STRIDE + (STRIDE - 1)
    within = jnp.arange(BLOCK, dtype=jnp.int32)
    causal = within[:, None] >= within[None, :]

    def block_inputs(block_index):
        row_start = (block_index * BLOCK).astype(jnp.int32)
        query_blk = lax.dynamic_slice_in_dim(queries, row_start, BLOCK, 0).reshape(BLOCK, HEADS, DH)
        key_blk = lax.dynamic_slice_in_dim(keys, row_start, BLOCK, 0).reshape(BLOCK, HEADS, DH)
        value_blk = lax.dynamic_slice_in_dim(values, row_start, BLOCK, 0).reshape(BLOCK, HEADS, DH)
        keys_all = jnp.concatenate([key_blk, panel_k], axis=0)
        values_all = jnp.concatenate([value_blk, panel_v], axis=0)
        reachable = panel_pos < row_start
        allowed = jnp.concatenate([causal, jnp.broadcast_to(reachable[None, :], (BLOCK, panel_count))], axis=1)[None]
        return (row_start, query_blk, keys_all, values_all, allowed)

    def forward_block(block_index):
        row_start, query_blk, keys_all, values_all, allowed = block_inputs(block_index)
        soft_weights = block_probs(query_blk, keys_all, allowed, scaling)
        mixture = jnp.einsum('hqk,khe->qhe', widen(soft_weights), values_all.astype(jnp.float32))
        return mixture.reshape(BLOCK, D).astype(jnp.bfloat16)
    block_ids = jnp.arange(TOKENS // BLOCK, dtype=jnp.int32)
    attended = lax.map(forward_block, block_ids).reshape(TOKENS, D)
    ext_all = jnp.concatenate([attended, attended[:OFFMAX]], axis=0)
    positions = jnp.arange(TOKENS, dtype=jnp.int32)
    weight_all = (1.0 + 2.0 * positions.astype(jnp.float32) / TOKENS) / TOKENS
    local_rows = jnp.arange(ROWS, dtype=jnp.int32)

    def slab_terms(slab_index):
        row_start = (slab_index * ROWS).astype(jnp.int32)
        extended = lax.dynamic_slice_in_dim(ext_all, row_start, ROWS + OFFMAX, 0)
        shifts = lax.dynamic_slice_in_dim(offsets, row_start, ROWS, 0)
        picked = lax.dynamic_slice_in_dim(negatives, row_start, ROWS, 0)
        weight = lax.dynamic_slice_in_dim(weight_all, row_start, ROWS, 0)
        gram_rows = jnp.dot(extended[:ROWS], extended.T, preferred_element_type=jnp.float32)
        wide_rows = widen(extended)
        squares = lax.optimization_barrier(jnp.sum(wide_rows * wide_rows, axis=1))
        target = local_rows + shifts
        return contrast(gram_rows[local_rows, target], gram_rows[local_rows[:, None], picked], squares, target, picked, weight, extended)
    loss_parts, grad_ext, grad_radius = lax.map(slab_terms, jnp.arange(TOKENS // ROWS, dtype=jnp.int32))
    grad_main = grad_ext[:, :ROWS].at[:, :OFFMAX].add(jnp.roll(grad_ext[:, ROWS:], 1, axis=0))
    radius_main = grad_radius[:, :ROWS].at[:, :OFFMAX].add(jnp.roll(grad_radius[:, ROWS:], 1, axis=0))
    attended_wide = widen(attended)
    radius_all = jnp.sqrt(lax.optimization_barrier(jnp.sum(attended_wide * attended_wide, axis=1)) / D + EPSILON)
    grad_att = grad_main.reshape(TOKENS, D) + (radius_main.reshape(TOKENS) / (D * radius_all))[:, None] * attended_wide
    grad_out = grad_att.astype(jnp.bfloat16)
    loss_value = jnp.sum(loss_parts)

    def backward_block(carried, block_index):
        panel_dk, panel_dv = carried
        row_start, query_blk, keys_all, values_all, allowed = block_inputs(block_index)
        grad_blk = widen(lax.dynamic_slice_in_dim(grad_out, row_start, BLOCK, 0)).reshape(BLOCK, HEADS, DH)
        out_blk = widen(lax.dynamic_slice_in_dim(attended, row_start, BLOCK, 0)).reshape(BLOCK, HEADS, DH)
        soft_weights = widen(block_probs(query_blk, keys_all, allowed, scaling))
        grad_prob = jnp.einsum('qhe,khe->hqk', grad_blk, values_all.astype(jnp.float32))
        delta_rows = jnp.transpose(lax.optimization_barrier(jnp.sum(grad_blk * out_blk, axis=2)))[:, :, None]
        grad_score = widen((soft_weights * (grad_prob - delta_rows)).astype(jnp.bfloat16))
        grad_query = jnp.einsum('hqk,khe->qhe', grad_score, keys_all.astype(jnp.float32)) * scaling
        grad_key = jnp.einsum('hqk,qhe->khe', grad_score, query_blk.astype(jnp.float32)) * scaling
        grad_value = jnp.einsum('hqk,qhe->khe', soft_weights, grad_blk)
        carried = (panel_dk + grad_key[BLOCK:], panel_dv + grad_value[BLOCK:])
        return (carried, (grad_query.reshape(BLOCK, D).astype(jnp.bfloat16), grad_key[:BLOCK].reshape(BLOCK, D), grad_value[:BLOCK].reshape(BLOCK, D)))
    zeros_panel = jnp.zeros((panel_count, HEADS, DH), jnp.float32)
    (panel_dk, panel_dv), (grad_q_all, grad_k_local, grad_v_local) = lax.scan(backward_block, (zeros_panel, zeros_panel), block_ids)
    grad_queries = grad_q_all.reshape(TOKENS, D)
    grad_keys = grad_k_local.reshape(panel_count, STRIDE, D).at[:, STRIDE - 1].add(panel_dk.reshape(panel_count, D))
    grad_values = grad_v_local.reshape(panel_count, STRIDE, D).at[:, STRIDE - 1].add(panel_dv.reshape(panel_count, D))
    return (grad_queries, grad_keys.reshape(TOKENS, D).astype(jnp.bfloat16), grad_values.reshape(TOKENS, D).astype(jnp.bfloat16), loss_value)
```

```python
import math

import jax
import jax.numpy as jnp
from jax import lax
from jax.experimental import pallas as pl
from jax.experimental.pallas import tpu as pltpu
from jax.sharding import PartitionSpec as P

DH = 128
D = 2048
ROWS = 512
FEAT = 256
STRIDE = 64
OFFMAX = 64
NZ = 4
NXY = 16
NSUB = 8
NSEQ = 64
TOKENS = 32768
PANEL = 1024

EPSILON = 1e-05
TEMPER = 0.1
MASKED = -1e30
SCALE = 1.0 / math.sqrt(DH)
SCALE2 = SCALE * math.log2(math.e)

F32 = jnp.float32
BF16 = jnp.bfloat16
I32 = jnp.int32
MESH = pl.DeviceIdType.MESH


def nn(a, b):
    return lax.dot_general(a, b, (((1,), (0,)), ((), ())), preferred_element_type=F32)


def nt(a, b):
    return lax.dot_general(a, b, (((1,), (1,)), ((), ())), preferred_element_type=F32)


def tn(a, b):
    return lax.dot_general(a, b, (((0,), (0,)), ((), ())), preferred_element_type=F32)


def iota(shape, dim):
    return lax.broadcasted_iota(I32, shape, dim)


def pick_lanes(x, index):
    return jnp.take_along_axis(x, index, axis=1, mode="promise_in_bounds")


def split(x):
    high = x.astype(BF16)
    return high, (x - high.astype(F32)).astype(BF16)


def kernel(
    q_ref, k_ref, v_ref, off_ref, neg_ref,
    dq_ref, dk_ref, dv_ref, loss_ref,
    gat, kblk, vblk, kblk_t, vblk_t, k_t, v_t, s_scr, p1, p2, o1, att, att_t, ahead,
    idx, idx_t, picked, pk_buf, sq_buf, coef, rcoef, ct_hi, ct_lo, h_hi, h_lo, grad_t,
    tail_out, tail_in, loss_xy, loss_z, gm, rs, rz_out, rz, dk_acc, dv_acc,
    z_sem, xy_sem, near_sem, pk_sem, sq_sem, lxy_sem, lz_sem, rs_sem, rz_sem,
):
    seq = lax.axis_index("seq").astype(I32)
    sub = lax.axis_index("sub").astype(I32)
    z, xy = lax.div(seq, NXY), lax.rem(seq, NXY)
    nxt, prv = lax.rem(seq + 1, NSEQ), lax.rem(seq + NSEQ - 1, NSEQ)

    def z_peer(j):
        return lax.rem(z + j, NZ) * NXY + xy

    def xy_peer(j):
        return z * NXY + lax.rem(xy + j, NXY)

    def sub_peer(j):
        return lax.rem(sub + j, NSUB)

    def remote(src, dst, sems, j, to_seq, to_sub):
        return pltpu.make_async_remote_copy(
            src_ref=src, dst_ref=dst, send_sem=sems.at[0, j], recv_sem=sems.at[1, j],
            device_id=(to_seq, to_sub), device_id_type=MESH,
        )

    def each(count, make, act):
        def body(j, carry):
            act(make(j))
            return carry

        lax.fori_loop(1, count, body, 0)

    def start(copy):
        copy.start()

    def finish(copy):
        copy.wait()

    barrier = pltpu.get_barrier_semaphore()

    def greet(to_seq, to_sub):
        pl.semaphore_signal(barrier, inc=1, device_id=(to_seq, to_sub), device_id_type=MESH)

    each(NZ, z_peer, lambda s: greet(s, sub))
    each(NXY, xy_peer, lambda s: greet(s, sub))
    each(NSUB, sub_peer, lambda u: greet(seq, u))
    greet(nxt, sub)
    greet(prv, sub)

    own_row = pl.multiple_of((xy * NZ + z) * 16, 16)
    chosen = (iota((16, ROWS), 1) == (iota((16, ROWS), 0) & 7) * STRIDE + (STRIDE - 1)).astype(F32).astype(BF16)
    first8 = iota((16, DH), 0) < 8
    k_sel = nn(chosen, k_ref[...])
    v_sel = nn(chosen, v_ref[...])
    gat[pl.ds(own_row, 16), :] = jnp.concatenate(
        [
            jnp.where(first8, k_sel[:, :DH], k_sel[:, DH:]),
            jnp.where(first8, v_sel[:, :DH], v_sel[:, DH:]),
        ],
        axis=1,
    ).astype(BF16)
    ahead[OFFMAX:, :] = jnp.zeros((128 - OFFMAX, FEAT), BF16)
    tail_in[OFFMAX:, :] = jnp.zeros((128 - OFFMAX, FEAT), BF16)

    pl.semaphore_wait(barrier, (NZ - 1) + (NXY - 1) + (NSUB - 1) + 2)

    def z_copy(j):
        tile = gat.at[pl.ds(own_row, 16), :]
        return remote(tile, tile, z_sem, j, z_peer(j), sub)

    block_row = pl.multiple_of(xy * 64, 64)

    def xy_copy(j):
        block = gat.at[pl.ds(block_row, 64), :]
        return remote(block, block, xy_sem, j, xy_peer(j), sub)

    each(NZ, z_copy, start)
    k_t[...] = k_ref[...].T
    v_t[...] = v_ref[...].T
    each(NZ, z_copy, finish)
    each(NXY, xy_copy, start)

    idx[...] = jnp.zeros((ROWS, 128), I32)
    idx[:, 0:15] = neg_ref[...]
    for b in range(4):
        rows = slice(b * 128, (b + 1) * 128)
        shift = jnp.broadcast_to(off_ref[b : b + 1, :], (128, 128)).T
        target = shift + iota((128, 128), 0) + b * 128
        both = jnp.where(iota((128, 128), 1) == 15, target, idx[rows, :])
        idx[rows, :] = both
        idx_t[:, rows] = both.T[0:16, :]

    lane_q = iota((64, ROWS), 1)
    row_k = iota((64, ROWS), 0)

    def rows64(i, base=0):
        return pl.ds(pl.multiple_of(base + i * 64, 64), 64)

    m1, l1 = [], []
    for h in range(2):
        cols = slice(h * DH, (h + 1) * DH)
        base = h * ROWS
        s_scr[base : base + ROWS, :] = nt(k_ref[:, cols], q_ref[:, cols])

        def top(i, best, base=base):
            x = s_scr[rows64(i, base), :]
            x = jnp.where(row_k + i * 64 <= lane_q, x, MASKED)
            s_scr[rows64(i, base), :] = x
            return jnp.maximum(best, jnp.max(x.reshape(8, 8, ROWS), axis=0))

        best = lax.fori_loop(0, 8, top, jnp.full((8, ROWS), MASKED, F32))
        level = jnp.max(best, axis=0, keepdims=True) * SCALE2

        def soft(i, total, base=base, level=level):
            p = jnp.exp2(s_scr[rows64(i, base), :] * SCALE2 - level)
            p1[rows64(i, base), :] = p.astype(BF16)
            return total + jnp.sum(p.reshape(8, 8, ROWS), axis=0)

        total = lax.fori_loop(0, 8, soft, jnp.zeros((8, ROWS), F32))
        m1.append(level)
        l1.append(jnp.sum(total, axis=0, keepdims=True))
        o1[cols, :] = nn(v_t[cols, :], p1[base : base + ROWS, :])

    each(NXY, xy_copy, finish)
    for b in range(4):
        rows = slice(b * 256, (b + 1) * 256)
        in_first = (iota((256, DH), 0) & 15) < 8
        one = jnp.where(in_first, 1.0, 0.0).astype(BF16)
        two = jnp.where(in_first, 0.0, 1.0).astype(BF16)
        in_first_t = (iota((DH, 256), 1) & 15) < 8
        one_t = jnp.where(in_first_t, 1.0, 0.0).astype(BF16)
        two_t = jnp.where(in_first_t, 0.0, 1.0).astype(BF16)
        for lanes, blk, blk_t in ((slice(0, DH), kblk, kblk_t), (slice(DH, FEAT), vblk, vblk_t)):
            tile = gat[rows, lanes]
            tile_t = tile.T
            blk[rows, 0:DH] = tile * one
            blk[rows, DH:FEAT] = tile * two
            blk_t[0:DH, rows] = tile_t * one_t
            blk_t[DH:FEAT, rows] = tile_t * two_t

    s_scr[...] = nt(kblk[...], q_ref[...])
    slot_z = lax.shift_right_logical(row_k, 4) * NXY

    def top2(i, best):
        x = s_scr[rows64(i), :]
        x = jnp.where(slot_z + i < seq, x, MASKED)
        s_scr[rows64(i), :] = x
        return jnp.maximum(best, jnp.max(x.reshape(4, 16, ROWS), axis=0))

    best = lax.fori_loop(0, NXY, top2, jnp.full((16, ROWS), MASKED, F32))
    m2 = [jnp.max(best[0:8], axis=0, keepdims=True) * SCALE2, jnp.max(best[8:16], axis=0, keepdims=True) * SCALE2]
    level16 = jnp.concatenate([jnp.broadcast_to(m2[0], (8, ROWS)), jnp.broadcast_to(m2[1], (8, ROWS))], axis=0)

    def soft2(i, total):
        p = jnp.exp2(s_scr[rows64(i), :].reshape(4, 16, ROWS) * SCALE2 - level16[None])
        p2[rows64(i), :] = p.reshape(64, ROWS).astype(BF16)
        return total + jnp.sum(p, axis=0)

    total = lax.fori_loop(0, NXY, soft2, jnp.zeros((16, ROWS), F32))
    l2 = [jnp.sum(total[0:8], axis=0, keepdims=True), jnp.sum(total[8:16], axis=0, keepdims=True)]
    o2 = nn(vblk_t[...], p2[...])
    w1, w2 = [], []
    squares = jnp.zeros((1, ROWS), F32)
    for h in range(2):
        cols = slice(h * DH, (h + 1) * DH)
        level = jnp.maximum(m1[h], m2[h])
        a1, a2 = jnp.exp2(m1[h] - level), jnp.exp2(m2[h] - level)
        inverse = 1.0 / (l1[h] * a1 + l2[h] * a2)
        w1.append(a1 * inverse)
        w2.append(a2 * inverse)
        out = (o1[cols, :] * w1[h] + o2[cols, :] * w2[h]).astype(BF16)
        att_t[cols, :] = out
        wide = out.astype(F32)
        squares = squares + jnp.sum(wide * wide, axis=0, keepdims=True)
    att[...] = att_t[...].T

    ahead_copy = remote(att.at[pl.ds(0, OFFMAX), :], ahead.at[pl.ds(0, OFFMAX), :], near_sem, 0, prv, sub)
    ahead_copy.start()
    s_scr[0:ROWS, :] = nn(att[...], att_t[...])

    def pick(i, carry):
        rows = rows64(i)
        here = idx[rows, :]
        low, high = here & 127, lax.shift_right_logical(here, 7)
        found = jnp.zeros((64, 128), F32)
        for b in range(4):
            value = pick_lanes(s_scr[rows, b * 128 : (b + 1) * 128], low)
            found = jnp.where(high == b, value, found)
        picked[rows, :] = found
        return carry

    lax.fori_loop(0, 8, pick, 0)
    ahead_copy.wait()
    late = slice(ROWS - 128, ROWS)
    far = nt(att[late, :], ahead[...])
    here = idx[late, :]
    picked[late, :] += jnp.where(lax.shift_right_logical(here, 7) == 4, pick_lanes(far, here & 127), 0.0)
    gram_ahead = nt(ahead[...], ahead[...])
    ahead_squares = jnp.sum(
        jnp.where(iota((128, 128), 0) == iota((128, 128), 1), gram_ahead, 0.0), axis=0, keepdims=True
    )

    pk_row = pl.multiple_of(sub * 16, 16)
    sq_row = pl.multiple_of(sub * 8, 8)
    for b in range(4):
        lanes = slice(b * 128, (b + 1) * 128)
        pk_buf[pl.ds(pk_row, 16), lanes] = picked[lanes, :].T[0:16, :].astype(BF16)
    sq_buf[pl.ds(sq_row, 8), :] = jnp.concatenate(
        [squares[:, b * 128 : (b + 1) * 128] for b in range(4)] + [ahead_squares, jnp.zeros((3, 128), F32)], axis=0
    )

    def sq_copy(j):
        part = sq_buf.at[pl.ds(sq_row, 8), :]
        return remote(part, part, sq_sem, j, seq, sub_peer(j))

    def pk_copy(j):
        part = pk_buf.at[pl.ds(pk_row, 16), :]
        return remote(part, part, pk_sem, j, seq, sub_peer(j))

    each(NSUB, sq_copy, start)
    each(NSUB, pk_copy, start)
    each(NSUB, sq_copy, finish)
    radius = jnp.sqrt(jnp.sum(sq_buf[...].reshape(NSUB, 8, 128), axis=0) / D + EPSILON)
    own_radius = jnp.concatenate([radius[b : b + 1, :] for b in range(4)], axis=1)
    parts = []
    for c in range(4):
        here = idx_t[:, c * 128 : (c + 1) * 128]
        low, high = here & 127, lax.shift_right_logical(here, 7)
        found = jnp.ones((16, 128), F32)
        for b in range(5 if c == 3 else 4):
            value = pick_lanes(jnp.broadcast_to(radius[b : b + 1, :], (16, 128)), low)
            found = jnp.where(high == b, value, found)
        parts.append(found)
    pair_radius = jnp.concatenate(parts, axis=1)
    factor = 1.0 / (D * TEMPER * own_radius * pair_radius)
    each(NSUB, pk_copy, finish)
    dots = jnp.sum(pk_buf[...].astype(F32).reshape(NSUB, 16, ROWS), axis=0)

    logits = dots * factor
    powers = jnp.exp(logits)
    expsum = jnp.sum(powers, axis=0, keepdims=True)
    step = (seq * ROWS + iota((1, ROWS), 1)).astype(F32)
    weight = (1.0 + 2.0 * step / TOKENS) / TOKENS
    first = (iota((16, ROWS), 0) == 15).astype(F32)
    loss_part = jnp.sum(weight * (jnp.log(expsum) - logits[15:16, :]), axis=1, keepdims=True)
    dlogits = (powers / expsum - first) * weight
    coef[...] = dlogits * factor
    pull = dlogits * logits
    rcoef[...] = pull / (D * pair_radius * pair_radius)
    own_pull = jnp.sum(pull, axis=0, keepdims=True) / (D * own_radius * own_radius)

    lxy_row = pl.multiple_of(xy * 8, 8)
    lz_row = pl.multiple_of(z * 8, 8)
    loss_xy[pl.ds(lxy_row, 8), :] = jnp.broadcast_to(loss_part, (8, 128))

    def lxy_copy(j):
        part = loss_xy.at[pl.ds(lxy_row, 8), :]
        return remote(part, part, lxy_sem, j, xy_peer(j), sub)

    def lz_copy(j):
        part = loss_z.at[pl.ds(lz_row, 8), :]
        return remote(part, part, lz_sem, j, z_peer(j), sub)

    each(NXY, lxy_copy, start)

    late_mark = iota((128, 128), 0) + ROWS == idx_t[15:16, late]
    far_c = jnp.where(late_mark, coef[15:16, late], 0.0)
    far_r = jnp.sum(jnp.where(late_mark, rcoef[15:16, late], 0.0), axis=1, keepdims=True)
    far_hi, far_lo = split(far_c)
    tail = nn(far_hi, att[late, :]) + nn(far_lo, att[late, :]) - far_r * ahead[...].astype(F32)
    tail_out[...] = tail.astype(BF16)
    tail_copy = remote(tail_out.at[pl.ds(0, OFFMAX), :], tail_in.at[pl.ds(0, OFFMAX), :], near_sem, 1, nxt, sub)
    tail_copy.start()

    row_c = iota((16, ROWS), 0)

    def table(i, carry):
        rows = pl.ds(pl.multiple_of(i * 16, 16), 16)
        here = row_c + i * 16
        pairs = jnp.zeros((16, ROWS), F32)
        pulls = jnp.zeros((16, ROWS), F32)
        for k in range(16):
            same = here == idx_t[k : k + 1, :]
            pairs = pairs + jnp.where(same, coef[k : k + 1, :], 0.0)
            pulls = pulls + jnp.where(same, rcoef[k : k + 1, :], 0.0)
        ct_hi[rows, :], ct_lo[rows, :] = split(pairs)
        h_hi[rows, :], h_lo[rows, :] = split(pulls)
        return carry

    lax.fori_loop(0, ROWS // 16, table, 0)
    ones = jnp.ones((16, ROWS), BF16)
    radial = nt(ones, h_hi[...])[0:1, :] + nt(ones, h_lo[...])[0:1, :] + own_pull
    mine = att_t[...]
    grad_t[...] = (
        nn(mine, ct_hi[...]) + nn(mine, ct_lo[...]) + nt(mine, ct_hi[...]) + nt(mine, ct_lo[...])
        - radial * mine.astype(F32)
    )
    grad_t[:, late] += tn(ahead[...], far_hi) + tn(ahead[...], far_lo)

    each(NXY, lxy_copy, finish)
    loss_z[pl.ds(lz_row, 8), :] = jnp.sum(loss_xy[...].reshape(NXY, 8, 128), axis=0)
    each(NZ, lz_copy, start)

    tail_copy.wait()
    grad_t[:, 0:128] += tail_in[...].astype(F32).T

    g1, g2, d1, d2 = [], [], [], []
    for h in range(2):
        cols = slice(h * DH, (h + 1) * DH)
        grad = grad_t[cols, :]
        wide = att_t[cols, :].astype(F32)
        one, two = (grad * w1[h]).astype(BF16), (grad * w2[h]).astype(BF16)
        g1.append(one)
        g2.append(two)
        d1.append(jnp.sum(one.astype(F32) * wide, axis=0, keepdims=True))
        d2.append(jnp.sum(two.astype(F32) * wide, axis=0, keepdims=True))
    both2 = jnp.concatenate(g2, axis=0)
    d16 = jnp.concatenate([jnp.broadcast_to(d2[0], (8, ROWS)), jnp.broadcast_to(d2[1], (8, ROWS))], axis=0)
    s_scr[...] = nn(vblk[...], both2)

    ds2 = kblk
    del ds2

    def slope2(i, carry):
        x = s_scr[rows64(i), :].reshape(4, 16, ROWS) - d16[None]
        p = p2[rows64(i), :].astype(F32).reshape(4, 16, ROWS)
        s_scr[rows64(i), :] = (x * p).reshape(64, ROWS)
        return carry

    lax.fori_loop(0, NXY, slope2, 0)
    slopes = s_scr[...].astype(BF16)
    in_first = (iota((PANEL, DH), 0) & 15) < 8
    key2 = nn(slopes, q_ref[...])
    gm[:, 0:DH] = (jnp.where(in_first, key2[:, :DH], key2[:, DH:]) * SCALE).astype(BF16)
    value2 = nt(p2[...], both2)
    gm[:, DH:FEAT] = jnp.where(in_first, value2[:, :DH], value2[:, DH:]).astype(BF16)

    def rs_copy(j):
        to = lax.rem(xy + j, NXY)
        return remote(
            gm.at[pl.ds(pl.multiple_of(to * 64, 64), 64), :], rs.at[pl.ds(block_row, 64), :],
            rs_sem, j, xy_peer(j), sub,
        )

    each(NXY, rs_copy, start)
    rs[pl.ds(block_row, 64), :] = gm[pl.ds(block_row, 64), :]
    query2 = nn(kblk_t[...], slopes)

    for h in range(2):
        cols = slice(h * DH, (h + 1) * DH)
        base = h * ROWS
        s_scr[base : base + ROWS, :] = nn(v_ref[:, cols], g1[h])

        def slope(i, carry, base=base, shift=d1[h]):
            x = s_scr[rows64(i, base), :] - shift
            s_scr[rows64(i, base), :] = x * p1[rows64(i, base), :].astype(F32)
            return carry

        lax.fori_loop(0, 8, slope, 0)
        near = s_scr[base : base + ROWS, :].astype(BF16)
        query = (nn(k_t[cols, :], near) + query2[cols, :]) * SCALE
        dq_ref[:, cols] = query.T.astype(BF16)
        dk_acc[:, cols] = nn(near, q_ref[:, cols]) * SCALE
        dv_acc[:, cols] = nt(p1[base : base + ROWS, :], g1[h])
    dk_ref[...] = dk_acc[...].astype(BF16)
    dv_ref[...] = dv_acc[...].astype(BF16)

    each(NZ, lz_copy, finish)
    loss_ref[...] = jnp.sum(loss_z[...].reshape(NZ, 8, 128), axis=0)
    each(NXY, rs_copy, finish)
    rz_out[...] = jnp.sum(rs[...].astype(F32).reshape(NXY, 64, FEAT), axis=0).astype(BF16)
    rz_row = pl.multiple_of(z * 16, 16)

    def rz_copy(j):
        to = lax.rem(z + j, NZ)
        return remote(
            rz_out.at[pl.ds(pl.multiple_of(to * 16, 16), 16), :], rz.at[pl.ds(rz_row, 16), :],
            rz_sem, j, z_peer(j), sub,
        )

    each(NZ, rz_copy, start)
    rz[pl.ds(rz_row, 16), :] = rz_out[pl.ds(rz_row, 16), :]
    each(NZ, rz_copy, finish)
    term = jnp.sum(rz[...].astype(F32).reshape(NZ, 16, FEAT), axis=0)
    last = iota((16, FEAT), 0) == 15
    for i in range(8):
        rows = slice(i * STRIDE + STRIDE - 16, (i + 1) * STRIDE)
        for acc, ref, lanes in ((dk_acc, dk_ref, slice(0, DH)), (dv_acc, dv_ref, slice(DH, FEAT))):
            extra = jnp.concatenate([term[i : i + 1, lanes], term[8 + i : 9 + i, lanes]], axis=1)
            ref[rows, :] = (acc[rows, :] + jnp.where(last, extra, 0.0)).astype(BF16)


def local(queries, keys, values, offsets, negatives):
    vmem = pl.BlockSpec(memory_space=pltpu.VMEM)
    wide = jax.ShapeDtypeStruct((ROWS, FEAT), BF16)

    def sems(count):
        return pltpu.SemaphoreType.DMA((2, count))

    outs = pl.pallas_call(
        kernel,
        out_shape=(wide, wide, wide, jax.ShapeDtypeStruct((8, 128), F32)),
        in_specs=[vmem] * 5,
        out_specs=(vmem,) * 4,
        scratch_shapes=[
            pltpu.VMEM((PANEL, FEAT), BF16),
            pltpu.VMEM((PANEL, FEAT), BF16),
            pltpu.VMEM((PANEL, FEAT), BF16),
            pltpu.VMEM((FEAT, PANEL), BF16),
            pltpu.VMEM((FEAT, PANEL), BF16),
            pltpu.VMEM((FEAT, ROWS), BF16),
            pltpu.VMEM((FEAT, ROWS), BF16),
            pltpu.VMEM((PANEL, ROWS), F32),
            pltpu.VMEM((PANEL, ROWS), BF16),
            pltpu.VMEM((PANEL, ROWS), BF16),
            pltpu.VMEM((FEAT, ROWS), F32),
            pltpu.VMEM((ROWS, FEAT), BF16),
            pltpu.VMEM((FEAT, ROWS), BF16),
            pltpu.VMEM((128, FEAT), BF16),
            pltpu.VMEM((ROWS, 128), I32),
            pltpu.VMEM((16, ROWS), I32),
            pltpu.VMEM((ROWS, 128), F32),
            pltpu.VMEM((NSUB * 16, ROWS), BF16),
            pltpu.VMEM((NSUB * 8, 128), F32),
            pltpu.VMEM((16, ROWS), F32),
            pltpu.VMEM((16, ROWS), F32),
            pltpu.VMEM((ROWS, ROWS), BF16),
            pltpu.VMEM((ROWS, ROWS), BF16),
            pltpu.VMEM((ROWS, ROWS), BF16),
            pltpu.VMEM((ROWS, ROWS), BF16),
            pltpu.VMEM((FEAT, ROWS), F32),
            pltpu.VMEM((128, FEAT), BF16),
            pltpu.VMEM((128, FEAT), BF16),
            pltpu.VMEM((NXY * 8, 128), F32),
            pltpu.VMEM((NZ * 8, 128), F32),
            pltpu.VMEM((PANEL, FEAT), BF16),
            pltpu.VMEM((PANEL, FEAT), BF16),
            pltpu.VMEM((64, FEAT), BF16),
            pltpu.VMEM((64, FEAT), BF16),
            pltpu.VMEM((ROWS, FEAT), F32),
            pltpu.VMEM((ROWS, FEAT), F32),
            sems(NZ), sems(NXY), sems(2), sems(NSUB), sems(NSUB), sems(NXY), sems(NZ), sems(NXY), sems(NZ),
        ],
        compiler_params=pltpu.CompilerParams(
            collective_id=0, has_side_effects=True, vmem_limit_bytes=48 * 1024 * 1024
        ),
    )(queries, keys, values, offsets.reshape(4, 128), negatives)
    return outs[0], outs[1], outs[2], outs[3][0, 0]


def solution(mesh):
    placed = (P("seq", "sub"), P("seq", "sub"), P("seq", "sub"), P("seq"), P("seq", None))
    return jax.shard_map(
        local,
        mesh=mesh,
        in_specs=placed,
        out_specs=(P("seq", "sub"), P("seq", "sub"), P("seq", "sub"), P()),
        check_vma=False,
    )
```

```python
import math

import jax
import jax.numpy as jnp
from jax import lax
from jax.experimental import pallas as pl
from jax.experimental.pallas import tpu as pltpu
from jax.sharding import PartitionSpec as P

DH = 128
D = 2048
ROWS = 512
FEAT = 256
STRIDE = 64
OFFMAX = 64
NZ = 4
NXY = 16
NSUB = 8
NSEQ = 64
TOKENS = 32768
PANEL = 1024
WIDE = 640

EPSILON = 1e-05
TEMPER = 0.1
MASKED = -1e30
SCALE = 1.0 / math.sqrt(DH)
SCALE2 = SCALE * math.log2(math.e)

F32 = jnp.float32
BF16 = jnp.bfloat16
I32 = jnp.int32
MESH = pl.DeviceIdType.MESH


def nn(a, b):
    return lax.dot_general(a, b, (((1,), (0,)), ((), ())), preferred_element_type=F32)


def nt(a, b):
    return lax.dot_general(a, b, (((1,), (1,)), ((), ())), preferred_element_type=F32)


def tn(a, b):
    return lax.dot_general(a, b, (((0,), (0,)), ((), ())), preferred_element_type=F32)


def iota(shape, dim):
    return lax.broadcasted_iota(I32, shape, dim)


def pick_lanes(x, index):
    return jnp.take_along_axis(x, index, axis=1, mode="promise_in_bounds")


def split(x):
    high = x.astype(BF16)
    return high, (x - high.astype(F32)).astype(BF16)


def kernel(
    q_hbm, k_hbm, v_hbm, off_hbm, neg_hbm,
    dq_ref, dk_ref, dv_ref, loss_ref,
    q, k, v, off, neg, kx, vx, gat, kblk, vblk, kblk_t, vblk_t, k_t, v_t, s_scr, p1, p2, o1, att, att_t,
    idx, idx_t, picked, pk_buf, sq_buf, coef, rcoef, ct_hi, ct_lo, radial, grad_t,
    tail_out, tail_in, loss_xy, loss_z, ds2, query2, gm, rs, rz_out, rz, own_term, dk_acc, dv_acc,
    load_sem, z_sem, own_sem, low_sem, mid_sem, near_sem, pk_sem, sq_sem, lxy_sem, lz_sem, rs_sem, rz_sem,
):
    seq = lax.axis_index("seq").astype(I32)
    sub = lax.axis_index("sub").astype(I32)
    z, xy = lax.div(seq, NXY), lax.rem(seq, NXY)
    nxt, prv = lax.rem(seq + 1, NSEQ), lax.rem(seq + NSEQ - 1, NSEQ)

    def z_seq(to):
        return to * NXY + xy

    def xy_peer(j):
        return z * NXY + lax.rem(xy + j, NXY)

    def sub_peer(j):
        return lax.rem(sub + j, NSUB)

    def remote(src, dst, sems, j, to_seq, to_sub):
        return pltpu.make_async_remote_copy(
            src_ref=src, dst_ref=dst, send_sem=sems.at[0, j], recv_sem=sems.at[1, j],
            device_id=(to_seq, to_sub), device_id_type=MESH,
        )

    def each(count, make, act):
        def body(j, carry):
            act(make(j))
            return carry

        lax.fori_loop(1, count, body, 0)

    def start(copy):
        copy.start()

    def finish(copy):
        copy.wait()

    loads = [
        pltpu.make_async_copy(src, dst, load_sem.at[i])
        for i, (src, dst) in enumerate(
            [(k_hbm, k), (v_hbm, v), (q_hbm, q.at[pl.ds(0, ROWS), :]), (off_hbm, off), (neg_hbm, neg)]
        )
    ]
    for load in loads:
        load.start()

    gat[...] = jnp.zeros((NZ, NXY * 16, FEAT), BF16)
    rz[...] = jnp.zeros((NZ * 16, FEAT), BF16)
    tail_in[...] = jnp.zeros((128, FEAT), BF16)
    barrier = pltpu.get_barrier_semaphore()

    def greet(to_seq, to_sub):
        pl.semaphore_signal(barrier, inc=1, device_id=(to_seq, to_sub), device_id_type=MESH)

    greet(z_seq(lax.rem(z + 1, NZ)), sub)
    greet(z_seq(lax.rem(z + 3, NZ)), sub)

    @pl.when(z < 2)
    def _():
        greet(z_seq(z + 2), sub)

    each(NXY, xy_peer, lambda to: greet(to, sub))
    greet(nxt, sub)
    greet(prv, sub)
    each(NSUB, sub_peer, lambda to: greet(seq, to))

    own_row = pl.multiple_of(xy * 16, 16)
    own_rows = pl.ds(own_row, 16)
    chosen = (iota((16, ROWS), 1) == (iota((16, ROWS), 0) & 7) * STRIDE + (STRIDE - 1)).astype(F32).astype(BF16)
    first8 = iota((16, DH), 0) < 8
    loads[0].wait()
    loads[1].wait()
    k_sel = nn(chosen, k[...])
    v_sel = nn(chosen, v[...])
    gat[z, own_rows, :] = jnp.concatenate(
        [
            jnp.where(first8, k_sel[:, :DH], k_sel[:, DH:]),
            jnp.where(first8, v_sel[:, :DH], v_sel[:, DH:]),
        ],
        axis=1,
    ).astype(BF16)
    loads[2].wait()
    q[ROWS + OFFMAX :, :] = jnp.zeros((WIDE - ROWS - OFFMAX, FEAT), BF16)

    pl.semaphore_wait(barrier, 2 + (NXY - 1) + 2 + (NSUB - 1) + lax.div(z, 2))

    pair = gat.at[pl.ds(0, 2), own_rows, :]
    mine_tile = gat.at[z, own_rows, :]

    def swap():
        return remote(mine_tile, mine_tile, z_sem, 0, z_seq(1 - z), sub)

    def relay(to):
        return remote(pair, pair, z_sem, 1, z_seq(to), sub)

    def third():
        tile = gat.at[2, own_rows, :]
        return remote(tile, tile, z_sem, 2, z_seq(3), sub)

    def own_copy(j):
        return remote(mine_tile, mine_tile, own_sem, j, xy_peer(j), sub)

    def low_copy(count):
        part = gat.at[pl.ds(0, count), own_rows, :]
        return lambda j: remote(part, part, low_sem, j, xy_peer(j), sub)

    def mid_copy(j):
        part = gat.at[2, own_rows, :]
        return remote(part, part, mid_sem, j, xy_peer(j), sub)

    @pl.when(z < 2)
    def _():
        swap().start()

    @pl.when(z == 2)
    def _():
        third().start()

    each(NXY, own_copy, start)
    near = [
        remote(q.at[pl.ds(0, OFFMAX), :], q.at[pl.ds(ROWS, OFFMAX), :], near_sem, 0, prv, sub),
        remote(k.at[pl.ds(0, OFFMAX), :], kx, near_sem, 1, prv, sub),
        remote(v.at[pl.ds(0, OFFMAX), :], vx, near_sem, 2, prv, sub),
    ]
    for copy in near:
        copy.start()

    @pl.when(z == 0)
    def _():
        swap().wait()
        relay(3).start()

    @pl.when(z == 1)
    def _():
        swap().wait()
        relay(2).start()
        each(NXY, low_copy(1), start)

    @pl.when(z == 2)
    def _():
        relay(2).wait_recv()
        each(NXY, low_copy(2), start)

    @pl.when(z == 3)
    def _():
        third().wait_recv()
        each(NXY, mid_copy, start)
        relay(3).wait_recv()
        each(NXY, low_copy(2), start)

    loads[3].wait()
    loads[4].wait()
    k_t[...] = k[...].T
    v_t[...] = v[...].T
    idx_t[0:15, :] = neg[...]
    for b in range(4):
        cols = slice(b * 128, (b + 1) * 128)
        idx_t[15:16, cols] = off[b : b + 1, :] + iota((1, 128), 1) + b * 128
    for b in range(4):
        cols = slice(b * 128, (b + 1) * 128)
        idx[cols, :] = jnp.concatenate([idx_t[:, cols], jnp.zeros((112, 128), I32)], axis=0).T

    lane_q = iota((64, ROWS), 1)
    row_k = iota((64, ROWS), 0)

    def rows64(i, base=0):
        return pl.ds(pl.multiple_of(base + i * 64, 64), 64)

    m1, l1 = [], []
    for h in range(2):
        cols = slice(h * DH, (h + 1) * DH)
        base = h * ROWS
        s_scr[base : base + ROWS, 0:ROWS] = nt(k[:, cols], q[0:ROWS, cols])

        def top(i, best, base=base):
            x = s_scr[rows64(i, base), 0:ROWS]
            x = jnp.where(row_k + i * 64 <= lane_q, x, MASKED)
            s_scr[rows64(i, base), 0:ROWS] = x
            return jnp.maximum(best, jnp.max(x.reshape(8, 8, ROWS), axis=0))

        best = lax.fori_loop(0, 8, top, jnp.full((8, ROWS), MASKED, F32))
        level = jnp.max(best, axis=0, keepdims=True) * SCALE2

        def soft(i, total, base=base, level=level):
            p = jnp.exp2(s_scr[rows64(i, base), 0:ROWS] * SCALE2 - level)
            p1[rows64(i, base), :] = p.astype(BF16)
            return total + jnp.sum(p.reshape(8, 8, ROWS), axis=0)

        total = lax.fori_loop(0, 8, soft, jnp.zeros((8, ROWS), F32))
        m1.append(level)
        l1.append(jnp.sum(total, axis=0, keepdims=True))
        o1[cols, 0:ROWS] = nn(v_t[cols, :], p1[base : base + ROWS, :])
    for copy in near:
        copy.wait()
    for h in range(2):
        cols = slice(h * DH, (h + 1) * DH)
        x = nt(kx[:, cols], q[ROWS:WIDE, cols])
        x = jnp.where(iota((64, 128), 0) <= iota((64, 128), 1), x, MASKED)
        level = jnp.max(x, axis=0, keepdims=True) * SCALE2
        p = jnp.exp2(x * SCALE2 - level)
        m1[h] = jnp.concatenate([m1[h], level], axis=1)
        l1[h] = jnp.concatenate([l1[h], jnp.sum(p, axis=0, keepdims=True)], axis=1)
        o1[cols, ROWS:WIDE] = tn(vx[:, cols], p.astype(BF16))

    each(NXY, own_copy, finish)

    @pl.when(z == 1)
    def _():
        each(NXY, low_copy(1), finish)

    @pl.when(z == 2)
    def _():
        each(NXY, low_copy(2), finish)

    @pl.when(z == 3)
    def _():
        each(NXY, mid_copy, finish)
        each(NXY, low_copy(2), finish)

    in_first = (iota((256, DH), 0) & 15) < 8
    one = jnp.where(in_first, 1.0, 0.0).astype(BF16)
    two = jnp.where(in_first, 0.0, 1.0).astype(BF16)
    in_first_t = (iota((DH, 256), 1) & 15) < 8
    one_t = jnp.where(in_first_t, 1.0, 0.0).astype(BF16)
    two_t = jnp.where(in_first_t, 0.0, 1.0).astype(BF16)
    for b in range(NZ):
        rows = slice(b * 256, (b + 1) * 256)
        for lanes, blk, blk_t in ((slice(0, DH), kblk, kblk_t), (slice(DH, FEAT), vblk, vblk_t)):
            tile = gat[b, :, lanes]
            tile_t = tile.T
            blk[rows, 0:DH] = tile * one
            blk[rows, DH:FEAT] = tile * two
            blk_t[0:DH, rows] = tile_t * one_t
            blk_t[DH:FEAT, rows] = tile_t * two_t

    s_scr[...] = nt(kblk[...], q[...])
    slab = lax.shift_right_logical(iota((64, WIDE), 0), 4)
    limit = jnp.where(iota((1, WIDE), 1) < ROWS, seq, nxt)

    def top2(i, best):
        x = s_scr[rows64(i), :]
        x = jnp.where(slab + i * 4 < limit, x, MASKED)
        s_scr[rows64(i), :] = x
        return jnp.maximum(best, jnp.max(x.reshape(4, 16, WIDE), axis=0))

    best = lax.fori_loop(0, NXY, top2, jnp.full((16, WIDE), MASKED, F32))
    m2 = [jnp.max(best[0:8], axis=0, keepdims=True) * SCALE2, jnp.max(best[8:16], axis=0, keepdims=True) * SCALE2]
    level16 = jnp.concatenate([jnp.broadcast_to(m2[0], (8, WIDE)), jnp.broadcast_to(m2[1], (8, WIDE))], axis=0)

    def soft2(i, total):
        p = jnp.exp2(s_scr[rows64(i), :].reshape(4, 16, WIDE) * SCALE2 - level16[None])
        p2[rows64(i), :] = p.reshape(64, WIDE).astype(BF16)
        return total + jnp.sum(p, axis=0)

    total = lax.fori_loop(0, NXY, soft2, jnp.zeros((16, WIDE), F32))
    l2 = [jnp.sum(total[0:8], axis=0, keepdims=True), jnp.sum(total[8:16], axis=0, keepdims=True)]
    o2 = nn(vblk_t[...], p2[...])
    w1, w2 = [], []
    squares = jnp.zeros((1, WIDE), F32)
    for h in range(2):
        cols = slice(h * DH, (h + 1) * DH)
        level = jnp.maximum(m1[h], m2[h])
        a1, a2 = jnp.exp2(m1[h] - level), jnp.exp2(m2[h] - level)
        inverse = 1.0 / (l1[h] * a1 + l2[h] * a2)
        a1, a2 = a1 * inverse, a2 * inverse
        w1.append(a1[:, 0:ROWS])
        w2.append(a2[:, 0:ROWS])
        out = (o1[cols, :] * a1 + o2[cols, :] * a2).astype(BF16)
        att_t[cols, :] = out
        wide = out.astype(F32)
        squares = squares + jnp.sum(wide * wide, axis=0, keepdims=True)

    sq_row = pl.multiple_of(sub * 8, 8)
    sq_buf[pl.ds(sq_row, 8), :] = jnp.concatenate(
        [squares[:, b * 128 : (b + 1) * 128] for b in range(5)] + [jnp.zeros((3, 128), F32)], axis=0
    )

    def sq_copy(j):
        part = sq_buf.at[pl.ds(sq_row, 8), :]
        return remote(part, part, sq_sem, j, seq, sub_peer(j))

    each(NSUB, sq_copy, start)
    att[...] = att_t[...].T
    s_scr[0:ROWS, :] = nn(att[0:ROWS, :], att_t[...])

    def pick(i, carry):
        rows = rows64(i)
        here = idx[rows, :]
        low, high = here & 127, lax.shift_right_logical(here, 7)
        found = jnp.zeros((64, 128), F32)
        for b in range(5):
            value = pick_lanes(s_scr[rows, b * 128 : (b + 1) * 128], low)
            found = jnp.where(high == b, value, found)
        picked[rows, :] = found
        return carry

    lax.fori_loop(0, 8, pick, 0)
    pk_row = pl.multiple_of(sub * 16, 16)
    for b in range(4):
        lanes = slice(b * 128, (b + 1) * 128)
        pk_buf[pl.ds(pk_row, 16), lanes] = picked[lanes, :].T[0:16, :].astype(BF16)

    def pk_copy(j):
        part = pk_buf.at[pl.ds(pk_row, 16), :]
        return remote(part, part, pk_sem, j, seq, sub_peer(j))

    each(NSUB, pk_copy, start)
    each(NSUB, sq_copy, finish)
    radius = jnp.sqrt(jnp.sum(sq_buf[...].reshape(NSUB, 8, 128), axis=0) / D + EPSILON)
    own_radius = jnp.concatenate([radius[b : b + 1, :] for b in range(4)], axis=1)
    parts = []
    for c in range(4):
        here = idx_t[:, c * 128 : (c + 1) * 128]
        low, high = here & 127, lax.shift_right_logical(here, 7)
        found = jnp.ones((16, 128), F32)
        for b in range(5 if c == 3 else 4):
            value = pick_lanes(jnp.broadcast_to(radius[b : b + 1, :], (16, 128)), low)
            found = jnp.where(high == b, value, found)
        parts.append(found)
    pair_radius = jnp.concatenate(parts, axis=1)
    factor = 1.0 / (D * TEMPER * own_radius * pair_radius)
    pair_share = 1.0 / (D * pair_radius * pair_radius)
    own_share = 1.0 / (D * own_radius * own_radius)
    each(NSUB, pk_copy, finish)
    dots = jnp.sum(pk_buf[...].astype(F32).reshape(NSUB, 16, ROWS), axis=0)

    logits = dots * factor
    powers = jnp.exp(logits)
    expsum = jnp.sum(powers, axis=0, keepdims=True)
    step = (seq * ROWS + iota((1, ROWS), 1)).astype(F32)
    weight = (1.0 + 2.0 * step / TOKENS) / TOKENS
    first = (iota((16, ROWS), 0) == 15).astype(F32)
    dlogits = (powers / expsum - first) * weight
    coef[...] = dlogits * factor
    pull = dlogits * logits
    rcoef[...] = pull * pair_share
    own_pull = jnp.sum(pull, axis=0, keepdims=True) * own_share

    late = slice(ROWS - 128, ROWS)
    ahead = att[ROWS:WIDE, :]
    late_mark = iota((128, 128), 0) + ROWS == idx_t[15:16, late]
    far_c = jnp.where(late_mark, coef[15:16, late], 0.0)
    far_r = jnp.sum(jnp.where(late_mark, rcoef[15:16, late], 0.0), axis=1, keepdims=True)
    far_hi, far_lo = split(far_c)
    tail = nn(far_hi, att[late, :]) + nn(far_lo, att[late, :]) - far_r * ahead.astype(F32)
    tail_out[...] = tail.astype(BF16)
    tail_copy = remote(tail_out.at[pl.ds(0, OFFMAX), :], tail_in.at[pl.ds(0, OFFMAX), :], near_sem, 3, nxt, sub)
    tail_copy.start()

    loss_part = jnp.sum(weight * (jnp.log(expsum) - logits[15:16, :]), axis=1, keepdims=True)
    lxy_row = pl.multiple_of(xy * 8, 8)
    loss_xy[pl.ds(lxy_row, 8), :] = jnp.broadcast_to(loss_part, (8, 128))

    def lxy_copy(j):
        part = loss_xy.at[pl.ds(lxy_row, 8), :]
        return remote(part, part, lxy_sem, j, xy_peer(j), sub)

    each(NXY, lxy_copy, start)
    row_c = iota((16, ROWS), 0)

    def table(i, carry):
        rows = pl.ds(pl.multiple_of(i * 16, 16), 16)
        here = row_c + i * 16
        pairs = jnp.zeros((16, ROWS), F32)
        pulls = jnp.zeros((16, ROWS), F32)
        for k in range(16):
            same = here == idx_t[k : k + 1, :]
            pairs = pairs + jnp.where(same, coef[k : k + 1, :], 0.0)
            pulls = pulls + jnp.where(same, rcoef[k : k + 1, :], 0.0)
        ct_hi[rows, :], ct_lo[rows, :] = split(pairs)
        radial[rows, :] = jnp.sum(pulls, axis=1, keepdims=True)
        return carry

    lax.fori_loop(0, ROWS // 16, table, 0)
    rows_own = att[0:ROWS, :]
    cols_own = att_t[:, 0:ROWS]
    pushed = nn(ct_hi[...], rows_own) + nn(ct_lo[...], rows_own) - radial[...] * rows_own.astype(F32)
    grad_t[...] = nn(cols_own, ct_hi[...]) + nn(cols_own, ct_lo[...]) - own_pull * cols_own.astype(F32) + pushed.T
    grad_t[:, late] += tn(ahead, far_hi) + tn(ahead, far_lo)
    tail_copy.wait()
    grad_t[:, 0:128] += tail_in[...].astype(F32).T

    g1, g2, d1, d2 = [], [], [], []
    for h in range(2):
        cols = slice(h * DH, (h + 1) * DH)
        grad = grad_t[cols, :]
        wide = att_t[cols, 0:ROWS].astype(F32)
        one, two = (grad * w1[h]).astype(BF16), (grad * w2[h]).astype(BF16)
        g1.append(one)
        g2.append(two)
        d1.append(jnp.sum(one.astype(F32) * wide, axis=0, keepdims=True))
        d2.append(jnp.sum(two.astype(F32) * wide, axis=0, keepdims=True))
    both2 = jnp.concatenate(g2, axis=0)
    d16 = jnp.concatenate([jnp.broadcast_to(d2[0], (8, ROWS)), jnp.broadcast_to(d2[1], (8, ROWS))], axis=0)

    def rows256(w):
        return pl.ds(pl.multiple_of(w * 256, 256), 256)

    def rs_copy(w):
        def make(j):
            to = pl.ds(pl.multiple_of(lax.rem(xy + j, NXY) * 16, 16), 16)
            return remote(gm.at[w, to, :], rs.at[w, own_rows, :], rs_sem, w * NXY + j, xy_peer(j), sub)

        return make

    def wave(w, carry):
        rows = rows256(w)
        s_scr[0:256, 0:ROWS] = nn(vblk[rows, :], both2)

        def slope(i, carry):
            x = s_scr[rows64(i), 0:ROWS].reshape(4, 16, ROWS) - d16[None]
            here = rows64(i, w * 256)
            p = p2[here, 0:ROWS].astype(F32).reshape(4, 16, ROWS)
            ds2[here, :] = (x * p).reshape(64, ROWS).astype(BF16)
            return carry

        lax.fori_loop(0, 4, slope, 0)
        head0 = (iota((256, DH), 0) & 15) < 8
        key2 = nn(ds2[rows, :], q[0:ROWS, :])
        value2 = nt(p2[rows, 0:ROWS], both2)
        gm[w, :, 0:DH] = (jnp.where(head0, key2[:, :DH], key2[:, DH:]) * SCALE).astype(BF16)
        gm[w, :, DH:FEAT] = jnp.where(head0, value2[:, :DH], value2[:, DH:]).astype(BF16)
        each(NXY, rs_copy(w), start)
        rs[w, own_rows, :] = gm[w, own_rows, :]
        return carry

    lax.fori_loop(0, z + 1, wave, 0)

    each(NXY, lxy_copy, finish)
    plane_loss = jnp.sum(loss_xy[...].reshape(NXY, 8, 128), axis=0)
    loss_z[0:8, :] = plane_loss
    lz_first = remote(loss_z.at[pl.ds(0, 8), :], loss_z.at[pl.ds(8, 8), :], lz_sem, 0, z_seq(z + 1 - 2 * lax.rem(z, 2)), sub)
    lz_first.start()

    query2[...] = jnp.zeros((FEAT, ROWS), F32)

    def far_query(w, carry):
        query2[...] += nn(kblk_t[:, rows256(w)], ds2[rows256(w), :])
        return carry

    lax.fori_loop(0, z + 1, far_query, 0)
    for h in range(2):
        cols = slice(h * DH, (h + 1) * DH)
        base = h * ROWS
        s_scr[base : base + ROWS, 0:ROWS] = nn(v[:, cols], g1[h])

        def slope1(i, carry, base=base, shift=d1[h]):
            x = s_scr[rows64(i, base), 0:ROWS] - shift
            s_scr[rows64(i, base), 0:ROWS] = x * p1[rows64(i, base), :].astype(F32)
            return carry

        lax.fori_loop(0, 8, slope1, 0)
        close = s_scr[base : base + ROWS, 0:ROWS].astype(BF16)
        query = (nn(k_t[cols, :], close) + query2[cols, :]) * SCALE
        dq_ref[:, cols] = query.T.astype(BF16)
        dk_acc[:, cols] = nn(close, q[0:ROWS, cols]) * SCALE
        dv_acc[:, cols] = nt(p1[base : base + ROWS, :], g1[h])
    dk_ref[...] = dk_acc[...].astype(BF16)
    dv_ref[...] = dv_acc[...].astype(BF16)

    def plane_sum(w):
        each(NXY, rs_copy(w), finish)
        return jnp.sum(rs[w].astype(F32).reshape(NXY, 16, FEAT), axis=0)

    rz_row = pl.multiple_of(z * 16, 16)

    def rz_copy(w):
        part = pl.ds(pl.multiple_of(w * 16, 16), 16)
        return remote(rz_out.at[part, :], rz.at[pl.ds(rz_row, 16), :], rz_sem, z - w, z_seq(w), sub)

    def down(w, carry):
        rz_out[pl.ds(pl.multiple_of(w * 16, 16), 16), :] = plane_sum(w).astype(BF16)
        rz_copy(w).start()
        return carry

    lax.fori_loop(0, z, down, 0)
    own_term[...] = plane_sum(z)
    lz_first.wait()
    loss_z[16:24, :] = loss_z[0:8, :] + loss_z[8:16, :]
    lz_second = remote(loss_z.at[pl.ds(16, 8), :], loss_z.at[pl.ds(24, 8), :], lz_sem, 1, z_seq(3 - z), sub)
    lz_second.start()

    def sent(w, carry):
        rz_copy(w).wait_send()
        return carry

    lax.fori_loop(0, z, sent, 0)

    def arrived(j, carry):
        slot = pl.ds(pl.multiple_of((z + j) * 16, 16), 16)
        remote(rz_out.at[pl.ds(0, 16), :], rz.at[slot, :], rz_sem, j, z_seq(z + j), sub).wait_recv()
        return carry

    lax.fori_loop(1, NZ - z, arrived, 0)
    term = own_term[...] + jnp.sum(rz[...].astype(F32).reshape(NZ, 16, FEAT), axis=0)
    last = iota((16, FEAT), 0) == 15
    for i in range(8):
        rows = slice(i * STRIDE + STRIDE - 16, (i + 1) * STRIDE)
        for acc, ref, lanes in ((dk_acc, dk_ref, slice(0, DH)), (dv_acc, dv_ref, slice(DH, FEAT))):
            extra = jnp.concatenate([term[i : i + 1, lanes], term[8 + i : 9 + i, lanes]], axis=1)
            ref[rows, :] = (acc[rows, :] + jnp.where(last, extra, 0.0)).astype(BF16)
    lz_second.wait()
    loss_ref[...] = loss_z[16:24, :] + loss_z[24:32, :]

    @pl.when(z < 2)
    def _():
        relay(3).wait_send()

    @pl.when(z == 2)
    def _():
        third().wait_send()


def emit(dq, dk, dv, loss, dq_out, dk_out, dv_out, loss_out, sems):
    copies = [
        pltpu.make_async_copy(src, dst, sems.at[i])
        for i, (src, dst) in enumerate([(dq, dq_out), (dk, dk_out), (dv, dv_out)])
    ]
    for copy in copies:
        copy.start()
    loss_out[...] = loss[0:1, 0:1]
    for copy in copies:
        copy.wait()


def local(queries, keys, values, offsets, negatives):
    vmem = pl.BlockSpec(memory_space=pltpu.VMEM)
    anywhere = pl.BlockSpec(memory_space=pl.ANY)
    wide = jax.ShapeDtypeStruct((ROWS, FEAT), BF16)

    def sems(count):
        return pltpu.SemaphoreType.DMA((2, count))

    outs = pl.pallas_call(
        kernel,
        out_shape=(wide, wide, wide, jax.ShapeDtypeStruct((8, 128), F32)),
        in_specs=[anywhere] * 5,
        out_specs=(vmem,) * 4,
        scratch_shapes=[
            pltpu.VMEM((WIDE, FEAT), BF16),
            pltpu.VMEM((ROWS, FEAT), BF16),
            pltpu.VMEM((ROWS, FEAT), BF16),
            pltpu.VMEM((4, 128), I32),
            pltpu.VMEM((15, ROWS), I32),
            pltpu.VMEM((OFFMAX, FEAT), BF16),
            pltpu.VMEM((OFFMAX, FEAT), BF16),
            pltpu.VMEM((NZ, NXY * 16, FEAT), BF16),
            pltpu.VMEM((PANEL, FEAT), BF16),
            pltpu.VMEM((PANEL, FEAT), BF16),
            pltpu.VMEM((FEAT, PANEL), BF16),
            pltpu.VMEM((FEAT, PANEL), BF16),
            pltpu.VMEM((FEAT, ROWS), BF16),
            pltpu.VMEM((FEAT, ROWS), BF16),
            pltpu.VMEM((PANEL, WIDE), F32),
            pltpu.VMEM((PANEL, ROWS), BF16),
            pltpu.VMEM((PANEL, WIDE), BF16),
            pltpu.VMEM((FEAT, WIDE), F32),
            pltpu.VMEM((WIDE, FEAT), BF16),
            pltpu.VMEM((FEAT, WIDE), BF16),
            pltpu.VMEM((ROWS, 128), I32),
            pltpu.VMEM((16, ROWS), I32),
            pltpu.VMEM((ROWS, 128), F32),
            pltpu.VMEM((NSUB * 16, ROWS), BF16),
            pltpu.VMEM((NSUB * 8, 128), F32),
            pltpu.VMEM((16, ROWS), F32),
            pltpu.VMEM((16, ROWS), F32),
            pltpu.VMEM((ROWS, ROWS), BF16),
            pltpu.VMEM((ROWS, ROWS), BF16),
            pltpu.VMEM((ROWS, 1), F32),
            pltpu.VMEM((FEAT, ROWS), F32),
            pltpu.VMEM((128, FEAT), BF16),
            pltpu.VMEM((128, FEAT), BF16),
            pltpu.VMEM((NXY * 8, 128), F32),
            pltpu.VMEM((32, 128), F32),
            pltpu.VMEM((PANEL, ROWS), BF16),
            pltpu.VMEM((FEAT, ROWS), F32),
            pltpu.VMEM((NZ, NXY * 16, FEAT), BF16),
            pltpu.VMEM((NZ, NXY * 16, FEAT), BF16),
            pltpu.VMEM((NZ * 16, FEAT), BF16),
            pltpu.VMEM((NZ * 16, FEAT), BF16),
            pltpu.VMEM((16, FEAT), F32),
            pltpu.VMEM((ROWS, FEAT), F32),
            pltpu.VMEM((ROWS, FEAT), F32),
            pltpu.SemaphoreType.DMA((5,)),
            sems(3), sems(NXY), sems(NXY), sems(NXY), sems(4), sems(NSUB), sems(NSUB), sems(NXY), sems(2),
            sems(NZ * NXY), sems(NZ),
        ],
        compiler_params=pltpu.CompilerParams(
            collective_id=0, has_side_effects=True, vmem_limit_bytes=54400 * 1024
        ),
    )(queries, keys, values, offsets.reshape(4, 128), negatives.T)
    dq, dk, dv, loss = pl.pallas_call(
        emit,
        out_shape=(wide, wide, wide, jax.ShapeDtypeStruct((1, 1), F32)),
        in_specs=[anywhere] * 3 + [vmem],
        out_specs=(anywhere, anywhere, anywhere, vmem),
        scratch_shapes=[pltpu.SemaphoreType.DMA((3,))],
        compiler_params=pltpu.CompilerParams(vmem_limit_bytes=1024 * 1024),
    )(*outs)
    return dq, dk, dv, loss.reshape(())


def solution(mesh):
    placed = (P("seq", "sub"), P("seq", "sub"), P("seq", "sub"), P("seq"), P("seq", None))
    return jax.shard_map(
        local,
        mesh=mesh,
        in_specs=placed,
        out_specs=(P("seq", "sub"), P("seq", "sub"), P("seq", "sub"), P()),
        check_vma=False,
    )
```

```python
import math

import jax
import jax.numpy as jnp
from jax import lax
from jax.experimental import pallas as pl
from jax.experimental.pallas import tpu as pltpu
from jax.sharding import PartitionSpec as P

DH = 128
D = 2048
ROWS = 512
FEAT = 256
STRIDE = 64
OFFMAX = 64
NZ = 4
NXY = 16
NSUB = 8
NSEQ = 64
TOKENS = 32768
PANEL = 1024
WIDE = 640

EPSILON = 1e-05
TEMPER = 0.1
MASKED = -1e30
SCALE = 1.0 / math.sqrt(DH)
SCALE2 = SCALE * math.log2(math.e)

F32 = jnp.float32
BF16 = jnp.bfloat16
I32 = jnp.int32
MESH = pl.DeviceIdType.MESH


def nn(a, b):
    return lax.dot_general(a, b, (((1,), (0,)), ((), ())), preferred_element_type=F32)


def nt(a, b):
    return lax.dot_general(a, b, (((1,), (1,)), ((), ())), preferred_element_type=F32)


def tn(a, b):
    return lax.dot_general(a, b, (((0,), (0,)), ((), ())), preferred_element_type=F32)


def iota(shape, dim):
    return lax.broadcasted_iota(I32, shape, dim)


def pick_lanes(x, index):
    return jnp.take_along_axis(x, index, axis=1, mode="promise_in_bounds")


def split(x):
    high = x.astype(BF16)
    return high, (x - high.astype(F32)).astype(BF16)


def kernel(
    q_hbm, k_hbm, v_hbm, off_hbm, neg_hbm,
    dq_ref, dk_ref, dv_ref, loss_ref,
    q, k, v, off, neg, kx, vx, gat, kblk, vblk, kblk_t, vblk_t, k_t, v_t, s_scr, p1, p2, o1, att, att_t,
    idx, idx_t, picked, pk_buf, sq_buf, coef, rcoef, ct_hi, ct_lo, radial, grad_t,
    tail_out, tail_in, loss_xy, loss_z, out1, out2, delta, k_part, v_part, ds2, query2, gm, rs, rz_out, rz, own_term, dk_acc, dv_acc,
    load_sem, z_sem, own_sem, low_sem, mid_sem, near_sem, pk_sem, sq_sem, lxy_sem, lz_sem, rs_sem, plane_sem, rz_sem,
):
    seq = lax.axis_index("seq").astype(I32)
    sub = lax.axis_index("sub").astype(I32)
    z, xy = lax.div(seq, NXY), lax.rem(seq, NXY)
    nxt, prv = lax.rem(seq + 1, NSEQ), lax.rem(seq + NSEQ - 1, NSEQ)

    def z_seq(to):
        return to * NXY + xy

    def xy_peer(j):
        return z * NXY + lax.rem(xy + j, NXY)

    def sub_peer(j):
        return lax.rem(sub + j, NSUB)

    def remote(src, dst, sems, j, to_seq, to_sub):
        return pltpu.make_async_remote_copy(
            src_ref=src, dst_ref=dst, send_sem=sems.at[0, j], recv_sem=sems.at[1, j],
            device_id=(to_seq, to_sub), device_id_type=MESH,
        )

    def drain(ref, sems, i):
        whole = remote(ref, ref, sems, i, prv, sub)
        whole.wait_send()
        whole.wait_recv()

    def each(count, make, act):
        def body(j, carry):
            act(make(j))
            return carry

        lax.fori_loop(1, count, body, 0)

    def start(copy):
        copy.start()

    def finish(copy):
        copy.wait()

    loads = [
        pltpu.make_async_copy(src, dst, load_sem.at[i])
        for i, (src, dst) in enumerate(
            [(k_hbm, k), (v_hbm, v), (q_hbm, q.at[pl.ds(0, ROWS), :]), (off_hbm, off), (neg_hbm, neg)]
        )
    ]
    for load in loads:
        load.start()

    gat[...] = jnp.zeros((NZ, NXY * 16, FEAT), BF16)
    rz[...] = jnp.zeros((NZ * 16, FEAT), BF16)
    rs[z] = jnp.zeros((NXY * 16, FEAT), BF16)
    tail_in[...] = jnp.zeros((128, FEAT), BF16)
    barrier = pltpu.get_barrier_semaphore()

    def greet(to_seq, to_sub):
        pl.semaphore_signal(barrier, inc=1, device_id=(to_seq, to_sub), device_id_type=MESH)

    greet(z_seq(lax.rem(z + 1, NZ)), sub)
    greet(z_seq(lax.rem(z + 3, NZ)), sub)

    @pl.when(z < 2)
    def _():
        greet(z_seq(z + 2), sub)

    each(NXY, xy_peer, lambda to: greet(to, sub))
    greet(nxt, sub)
    greet(prv, sub)
    each(NSUB, sub_peer, lambda to: greet(seq, to))

    own_row = pl.multiple_of(xy * 16, 16)
    own_rows = pl.ds(own_row, 16)
    chosen = (iota((16, ROWS), 1) == (iota((16, ROWS), 0) & 7) * STRIDE + (STRIDE - 1)).astype(F32).astype(BF16)
    first8 = iota((16, DH), 0) < 8
    loads[0].wait()
    loads[1].wait()
    k_sel = nn(chosen, k[...])
    v_sel = nn(chosen, v[...])
    gat[z, own_rows, :] = jnp.concatenate(
        [
            jnp.where(first8, k_sel[:, :DH], k_sel[:, DH:]),
            jnp.where(first8, v_sel[:, :DH], v_sel[:, DH:]),
        ],
        axis=1,
    ).astype(BF16)
    loads[2].wait()
    q[ROWS + OFFMAX :, :] = jnp.zeros((WIDE - ROWS - OFFMAX, FEAT), BF16)

    pl.semaphore_wait(barrier, 2 + (NXY - 1) + 2 + (NSUB - 1) + lax.div(z, 2))

    pair = gat.at[pl.ds(0, 2), own_rows, :]
    mine_tile = gat.at[z, own_rows, :]

    def swap():
        return remote(mine_tile, mine_tile, z_sem, 0, z_seq(1 - z), sub)

    def relay(to):
        return remote(pair, pair, z_sem, 1, z_seq(to), sub)

    def third():
        tile = gat.at[2, own_rows, :]
        return remote(tile, tile, z_sem, 2, z_seq(3), sub)

    def own_copy(j):
        return remote(mine_tile, mine_tile, own_sem, 0, xy_peer(j), sub)

    def low_copy(count):
        part = gat.at[pl.ds(0, count), own_rows, :]
        return lambda j: remote(part, part, low_sem, 0, xy_peer(j), sub)

    def mid_copy(j):
        part = gat.at[2, own_rows, :]
        return remote(part, part, mid_sem, 0, xy_peer(j), sub)

    @pl.when(z < 2)
    def _():
        swap().start()

    @pl.when(z == 2)
    def _():
        third().start()

    each(NXY, own_copy, start)
    near = [
        remote(q.at[pl.ds(0, OFFMAX), :], q.at[pl.ds(ROWS, OFFMAX), :], near_sem, 0, prv, sub),
        remote(k.at[pl.ds(0, OFFMAX), :], kx, near_sem, 1, prv, sub),
        remote(v.at[pl.ds(0, OFFMAX), :], vx, near_sem, 2, prv, sub),
    ]
    for copy in near:
        copy.start()

    @pl.when(z == 0)
    def _():
        swap().wait()
        relay(3).start()

    @pl.when(z == 1)
    def _():
        swap().wait()
        relay(2).start()
        each(NXY, low_copy(1), start)

    @pl.when(z == 2)
    def _():
        relay(2).wait_recv()
        each(NXY, low_copy(2), start)

    @pl.when(z == 3)
    def _():
        relay(3).wait_recv()
        each(NXY, low_copy(2), start)
        third().wait_recv()
        each(NXY, mid_copy, start)

    loads[3].wait()
    loads[4].wait()
    k_t[...] = k[...].T
    v_t[...] = v[...].T
    idx_t[0:15, :] = neg[...]
    for b in range(4):
        cols = slice(b * 128, (b + 1) * 128)
        idx_t[15:16, cols] = off[b : b + 1, :] + iota((1, 128), 1) + b * 128
    for b in range(4):
        cols = slice(b * 128, (b + 1) * 128)
        idx[cols, :] = jnp.concatenate([idx_t[:, cols], jnp.zeros((112, 128), I32)], axis=0).T

    lane_q = iota((64, ROWS), 1)
    row_k = iota((64, ROWS), 0)

    def rows64(i, base=0):
        return pl.ds(pl.multiple_of(base + i * 64, 64), 64)

    m1, l1 = [], []
    for h in range(2):
        cols = slice(h * DH, (h + 1) * DH)
        base = h * ROWS
        s_scr[base : base + ROWS, 0:ROWS] = nt(k[:, cols], q[0:ROWS, cols])

        def top(i, best, base=base):
            x = s_scr[rows64(i, base), 0:ROWS]
            x = jnp.where(row_k + i * 64 <= lane_q, x, MASKED)
            s_scr[rows64(i, base), 0:ROWS] = x
            return jnp.maximum(best, jnp.max(x.reshape(8, 8, ROWS), axis=0))

        best = lax.fori_loop(0, 8, top, jnp.full((8, ROWS), MASKED, F32))
        level = jnp.max(best, axis=0, keepdims=True) * SCALE2

        def soft(i, total, base=base, level=level):
            p = jnp.exp2(s_scr[rows64(i, base), 0:ROWS] * SCALE2 - level)
            p1[rows64(i, base), :] = p.astype(BF16)
            return total + jnp.sum(p.reshape(8, 8, ROWS), axis=0)

        total = lax.fori_loop(0, 8, soft, jnp.zeros((8, ROWS), F32))
        m1.append(level)
        l1.append(jnp.sum(total, axis=0, keepdims=True))
        o1[cols, 0:ROWS] = nn(v_t[cols, :], p1[base : base + ROWS, :])
    for copy in near:
        copy.wait()
    for h in range(2):
        cols = slice(h * DH, (h + 1) * DH)
        x = nt(kx[:, cols], q[ROWS:WIDE, cols])
        x = jnp.where(iota((64, 128), 0) <= iota((64, 128), 1), x, MASKED)
        level = jnp.max(x, axis=0, keepdims=True) * SCALE2
        p = jnp.exp2(x * SCALE2 - level)
        m1[h] = jnp.concatenate([m1[h], level], axis=1)
        l1[h] = jnp.concatenate([l1[h], jnp.sum(p, axis=0, keepdims=True)], axis=1)
        o1[cols, ROWS:WIDE] = tn(vx[:, cols], p.astype(BF16))

    others = pl.ds(0, (NXY - 1) * 16)
    drain(gat.at[z, others, :], own_sem, 0)

    @pl.when(z == 1)
    def _():
        drain(gat.at[pl.ds(0, 1), others, :], low_sem, 0)

    @pl.when(z == 2)
    def _():
        drain(gat.at[pl.ds(0, 2), others, :], low_sem, 0)

    @pl.when(z == 3)
    def _():
        drain(gat.at[2, others, :], mid_sem, 0)
        drain(gat.at[pl.ds(0, 2), others, :], low_sem, 0)

    in_first = (iota((256, DH), 0) & 15) < 8
    one = jnp.where(in_first, 1.0, 0.0).astype(BF16)
    two = jnp.where(in_first, 0.0, 1.0).astype(BF16)
    in_first_t = (iota((DH, 256), 1) & 15) < 8
    one_t = jnp.where(in_first_t, 1.0, 0.0).astype(BF16)
    two_t = jnp.where(in_first_t, 0.0, 1.0).astype(BF16)
    for b in range(NZ):
        rows = slice(b * 256, (b + 1) * 256)
        for lanes, blk, blk_t in ((slice(0, DH), kblk, kblk_t), (slice(DH, FEAT), vblk, vblk_t)):
            tile = gat[b, :, lanes]
            tile_t = tile.T
            blk[rows, 0:DH] = tile * one
            blk[rows, DH:FEAT] = tile * two
            blk_t[0:DH, rows] = tile_t * one_t
            blk_t[DH:FEAT, rows] = tile_t * two_t

    s_scr[...] = nt(kblk[...], q[...])
    slab = lax.shift_right_logical(iota((64, WIDE), 0), 4)
    limit = jnp.where(iota((1, WIDE), 1) < ROWS, seq, nxt)

    def top2(i, best):
        x = s_scr[rows64(i), :]
        x = jnp.where(slab + i * 4 < limit, x, MASKED)
        s_scr[rows64(i), :] = x
        return jnp.maximum(best, jnp.max(x.reshape(4, 16, WIDE), axis=0))

    best = lax.fori_loop(0, NXY, top2, jnp.full((16, WIDE), MASKED, F32))
    m2 = [jnp.max(best[0:8], axis=0, keepdims=True) * SCALE2, jnp.max(best[8:16], axis=0, keepdims=True) * SCALE2]
    level16 = jnp.concatenate([jnp.broadcast_to(m2[0], (8, WIDE)), jnp.broadcast_to(m2[1], (8, WIDE))], axis=0)

    def soft2(i, total):
        p = jnp.exp2(s_scr[rows64(i), :].reshape(4, 16, WIDE) * SCALE2 - level16[None])
        p2[rows64(i), :] = p.reshape(64, WIDE).astype(BF16)
        return total + jnp.sum(p, axis=0)

    total = lax.fori_loop(0, NXY, soft2, jnp.zeros((16, WIDE), F32))
    l2 = [jnp.sum(total[0:8], axis=0, keepdims=True), jnp.sum(total[8:16], axis=0, keepdims=True)]
    o2 = nn(vblk_t[...], p2[...])
    w1, w2 = [], []
    squares = jnp.zeros((1, WIDE), F32)
    for h in range(2):
        cols = slice(h * DH, (h + 1) * DH)
        level = jnp.maximum(m1[h], m2[h])
        a1, a2 = jnp.exp2(m1[h] - level), jnp.exp2(m2[h] - level)
        inverse = 1.0 / (l1[h] * a1 + l2[h] * a2)
        a1, a2 = a1 * inverse, a2 * inverse
        w1.append(a1[:, 0:ROWS])
        w2.append(a2[:, 0:ROWS])
        out = (o1[cols, :] * a1 + o2[cols, :] * a2).astype(BF16)
        att_t[cols, :] = out
        wide = out.astype(F32)
        squares = squares + jnp.sum(wide * wide, axis=0, keepdims=True)

    sq_row = pl.multiple_of(sub * 8, 8)
    sq_buf[pl.ds(sq_row, 8), :] = jnp.concatenate(
        [squares[:, b * 128 : (b + 1) * 128] for b in range(5)] + [jnp.zeros((3, 128), F32)], axis=0
    )

    def sq_copy(j):
        part = sq_buf.at[pl.ds(sq_row, 8), :]
        return remote(part, part, sq_sem, 0, seq, sub_peer(j))

    each(NSUB, sq_copy, start)
    att[...] = att_t[...].T
    s_scr[0:ROWS, :] = nn(att[0:ROWS, :], att_t[...])

    def pick(i, carry):
        rows = rows64(i)
        here = idx[rows, :]
        low, high = here & 127, lax.shift_right_logical(here, 7)
        found = jnp.zeros((64, 128), F32)
        for b in range(5):
            value = pick_lanes(s_scr[rows, b * 128 : (b + 1) * 128], low)
            found = jnp.where(high == b, value, found)
        picked[rows, :] = found
        return carry

    lax.fori_loop(0, 8, pick, 0)
    pk_row = pl.multiple_of(sub * 16, 16)
    for b in range(4):
        lanes = slice(b * 128, (b + 1) * 128)
        pk_buf[pl.ds(pk_row, 16), lanes] = picked[lanes, :].T[0:16, :].astype(BF16)

    def pk_copy(j):
        part = pk_buf.at[pl.ds(pk_row, 16), :]
        return remote(part, part, pk_sem, 0, seq, sub_peer(j))

    each(NSUB, pk_copy, start)
    drain(sq_buf.at[pl.ds(0, (NSUB - 1) * 8), :], sq_sem, 0)
    radius = jnp.sqrt(jnp.sum(sq_buf[...].reshape(NSUB, 8, 128), axis=0) / D + EPSILON)
    own_radius = jnp.concatenate([radius[b : b + 1, :] for b in range(4)], axis=1)
    parts = []
    for c in range(4):
        here = idx_t[:, c * 128 : (c + 1) * 128]
        low, high = here & 127, lax.shift_right_logical(here, 7)
        found = jnp.ones((16, 128), F32)
        for b in range(5 if c == 3 else 4):
            value = pick_lanes(jnp.broadcast_to(radius[b : b + 1, :], (16, 128)), low)
            found = jnp.where(high == b, value, found)
        parts.append(found)
    pair_radius = jnp.concatenate(parts, axis=1)
    factor = 1.0 / (D * TEMPER * own_radius * pair_radius)
    pair_share = 1.0 / (D * pair_radius * pair_radius)
    own_share = 1.0 / (D * own_radius * own_radius)
    drain(pk_buf.at[pl.ds(0, (NSUB - 1) * 16), :], pk_sem, 0)
    dots = jnp.sum(pk_buf[...].astype(F32).reshape(NSUB, 16, ROWS), axis=0)

    logits = dots * factor
    powers = jnp.exp(logits)
    expsum = jnp.sum(powers, axis=0, keepdims=True)
    step = (seq * ROWS + iota((1, ROWS), 1)).astype(F32)
    weight = (1.0 + 2.0 * step / TOKENS) / TOKENS
    first = (iota((16, ROWS), 0) == 15).astype(F32)
    dlogits = (powers / expsum - first) * weight
    coef[...] = dlogits * factor
    pull = dlogits * logits
    rcoef[...] = pull * pair_share
    own_pull = jnp.sum(pull, axis=0, keepdims=True) * own_share

    late = slice(ROWS - 128, ROWS)
    ahead = att[ROWS:WIDE, :]
    late_mark = iota((128, 128), 0) + ROWS == idx_t[15:16, late]
    far_c = jnp.where(late_mark, coef[15:16, late], 0.0)
    far_r = jnp.sum(jnp.where(late_mark, rcoef[15:16, late], 0.0), axis=1, keepdims=True)
    far_hi, far_lo = split(far_c)
    tail = nn(far_hi, att[late, :]) + nn(far_lo, att[late, :]) - far_r * ahead.astype(F32)
    tail_out[...] = tail.astype(BF16)
    tail_copy = remote(tail_out.at[pl.ds(0, OFFMAX), :], tail_in.at[pl.ds(0, OFFMAX), :], near_sem, 3, nxt, sub)
    tail_copy.start()

    loss_part = jnp.sum(weight * (jnp.log(expsum) - logits[15:16, :]), axis=1, keepdims=True)
    lxy_row = pl.multiple_of(xy * 8, 8)
    loss_xy[pl.ds(lxy_row, 8), :] = jnp.broadcast_to(loss_part, (8, 128))

    def lxy_copy(j):
        part = loss_xy.at[pl.ds(lxy_row, 8), :]
        return remote(part, part, lxy_sem, 0, xy_peer(j), sub)

    each(NXY, lxy_copy, start)
    row_c = iota((16, ROWS), 0)

    def table(i, carry):
        rows = pl.ds(pl.multiple_of(i * 16, 16), 16)
        here = row_c + i * 16
        pairs = jnp.zeros((16, ROWS), F32)
        pulls = jnp.zeros((16, ROWS), F32)
        for k in range(16):
            same = here == idx_t[k : k + 1, :]
            pairs = pairs + jnp.where(same, coef[k : k + 1, :], 0.0)
            pulls = pulls + jnp.where(same, rcoef[k : k + 1, :], 0.0)
        ct_hi[rows, :], ct_lo[rows, :] = split(pairs)
        radial[rows, :] = pulls[:, 0:128] + pulls[:, 128:256] + pulls[:, 256:384] + pulls[:, 384:512]
        return carry

    lax.fori_loop(0, ROWS // 16, table, 0)
    rows_own = att[0:ROWS, :]
    radial_sum = jnp.sum(radial[...], axis=1, keepdims=True)
    cols_own = att_t[:, 0:ROWS]
    pushed = nn(ct_hi[...], rows_own) + nn(ct_lo[...], rows_own) - radial_sum * rows_own.astype(F32)
    grad_t[...] = nn(cols_own, ct_hi[...]) + nn(cols_own, ct_lo[...]) - own_pull * cols_own.astype(F32) + pushed.T
    grad_t[:, late] += tn(ahead, far_hi) + tn(ahead, far_lo)
    def scale(span):
        for h in range(2):
            cols = slice(h * DH, (h + 1) * DH)
            grad = grad_t[cols, span]
            wide = att_t[cols, span].astype(F32)
            one, two = (grad * w1[h][:, span]).astype(BF16), (grad * w2[h][:, span]).astype(BF16)
            out1[cols, span] = one
            out2[cols, span] = two
            delta[h : h + 1, span] = jnp.sum(one.astype(F32) * wide, axis=0, keepdims=True)
            delta[2 + h : 3 + h, span] = jnp.sum(two.astype(F32) * wide, axis=0, keepdims=True)

    def rows256(w):
        return pl.ds(pl.multiple_of(w * 256, 256), 256)

    def part(w, span, d16):
        rows = rows256(w)
        count = span.stop - span.start
        s_scr[0:256, span] = nn(vblk[rows, :], out2[:, span])

        def slope(i, carry):
            x = s_scr[rows64(i), span].reshape(4, 16, count) - d16[None]
            here = rows64(i, w * 256)
            p = p2[here, span].astype(F32).reshape(4, 16, count)
            ds2[here, span] = (x * p).reshape(64, count).astype(BF16)
            return carry

        lax.fori_loop(0, 4, slope, 0)
        return nn(ds2[rows, span], q[span, :]), nt(p2[rows, span], out2[:, span])

    def both_heads(span):
        count = span.stop - span.start
        return jnp.concatenate(
            [jnp.broadcast_to(delta[2:3, span], (8, count)), jnp.broadcast_to(delta[3:4, span], (8, count))], axis=0
        )

    most, few = slice(128, ROWS), slice(0, 128)
    scale(most)
    d_most = both_heads(most)

    def most_part(w, carry):
        rows = rows256(w)
        k_part[rows, :], v_part[rows, :] = part(w, most, d_most)
        return carry

    lax.fori_loop(0, z + 1, most_part, 0)
    tail_copy.wait()
    grad_t[:, few] += tail_in[...].astype(F32).T
    scale(few)
    d_few = both_heads(few)

    def rs_copy(w, sems, slot):
        def make(j):
            to = pl.ds(pl.multiple_of(lax.rem(xy + j, NXY) * 16, 16), 16)
            return remote(gm.at[w, to, :], rs.at[w, own_rows, :], sems, slot(j), xy_peer(j), sub)

        return make

    def wave(w, carry):
        rows = rows256(w)
        key2, value2 = part(w, few, d_few)
        key2 = key2 + k_part[rows, :]
        value2 = value2 + v_part[rows, :]
        head0 = (iota((256, DH), 0) & 15) < 8
        gm[w, :, 0:DH] = (jnp.where(head0, key2[:, :DH], key2[:, DH:]) * SCALE).astype(BF16)
        gm[w, :, DH:FEAT] = jnp.where(head0, value2[:, :DH], value2[:, DH:]).astype(BF16)

        rs[w, own_rows, :] = gm[w, own_rows, :]

        @pl.when(w < z)
        def _():
            each(NXY, rs_copy(w, rs_sem, lambda j: w), start)

        return carry

    lax.fori_loop(0, z + 1, wave, 0)

    plane_copy = rs_copy(z, plane_sem, lambda j: j)

    def send(j, carry):
        plane_copy(j).start()
        return carry

    lax.fori_loop(NXY - xy, NXY, send, 0)

    drain(loss_xy.at[pl.ds(0, (NXY - 1) * 8), :], lxy_sem, 0)
    plane_row = pl.ds(pl.multiple_of(z * 8, 8), 8)
    loss_z[plane_row, :] = jnp.sum(loss_xy[...].reshape(NXY, 8, 128), axis=0)

    def loss_swap():
        part = loss_z.at[plane_row, :]
        return remote(part, part, lz_sem, 0, z_seq(1 - z), sub)

    def loss_pair(to):
        part = loss_z.at[pl.ds(0, 16), :]
        return remote(part, part, lz_sem, 1, z_seq(to), sub)

    def loss_one(w, i, to):
        part = loss_z.at[pl.ds(w * 8, 8), :]
        return remote(part, part, lz_sem, i, z_seq(to), sub)

    def from2():
        return [loss_one(2, 2, 0), loss_one(2, 3, 1), loss_one(2, 4, 3)]

    def from3():
        return [loss_one(3, 5, 0), loss_one(3, 6, 1), loss_one(3, 7, 2)]

    @pl.when(z < 2)
    def _():
        loss_swap().start()

    @pl.when(z == 2)
    def _():
        for copy in from2():
            copy.start()

    @pl.when(z == 3)
    def _():
        for copy in from3():
            copy.start()

    query2[...] = jnp.zeros((FEAT, ROWS), F32)

    def far_query(w, carry):
        query2[...] += nn(kblk_t[:, rows256(w)], ds2[rows256(w), :])
        return carry

    lax.fori_loop(0, z + 1, far_query, 0)
    for h in range(2):
        cols = slice(h * DH, (h + 1) * DH)
        base = h * ROWS
        s_scr[base : base + ROWS, 0:ROWS] = nn(v[:, cols], out1[cols, :])

        def slope1(i, carry, base=base, h=h):
            x = s_scr[rows64(i, base), 0:ROWS] - delta[h : h + 1, :]
            s_scr[rows64(i, base), 0:ROWS] = x * p1[rows64(i, base), :].astype(F32)
            return carry

        lax.fori_loop(0, 8, slope1, 0)
        close = s_scr[base : base + ROWS, 0:ROWS].astype(BF16)
        query = (nn(k_t[cols, :], close) + query2[cols, :]) * SCALE
        dq_ref[:, cols] = query.T.astype(BF16)
        dk_acc[:, cols] = nn(close, q[0:ROWS, cols]) * SCALE
        dv_acc[:, cols] = nt(p1[base : base + ROWS, :], out1[cols, :])
    dk_ref[...] = dk_acc[...].astype(BF16)
    dv_ref[...] = dv_acc[...].astype(BF16)

    def plane_sum(w):
        return jnp.sum(rs[w].astype(F32).reshape(NXY, 16, FEAT), axis=0)

    rz_row = pl.multiple_of(z * 16, 16)

    def rz_copy(w):
        part = pl.ds(pl.multiple_of(w * 16, 16), 16)
        return remote(rz_out.at[part, :], rz.at[pl.ds(rz_row, 16), :], rz_sem, z - w, z_seq(w), sub)

    def down(w, carry):
        drain(rs.at[w, others, :], rs_sem, w)
        rz_out[pl.ds(pl.multiple_of(w * 16, 16), 16), :] = plane_sum(w).astype(BF16)
        rz_copy(w).start()
        return carry

    lax.fori_loop(0, z, down, 0)
    def plane_sent(j, carry):
        plane_copy(j).wait_send()
        return carry

    def plane_came(j, carry):
        plane_copy(j).wait_recv()
        return carry

    lax.fori_loop(xy + 1, NXY, plane_came, 0)
    lax.fori_loop(NXY - xy, NXY, plane_sent, 0)
    own_term[...] = plane_sum(z)

    @pl.when(z == 0)
    def _():
        loss_swap().wait()
        loss_pair(3).start()

    @pl.when(z == 1)
    def _():
        loss_swap().wait()
        loss_pair(2).start()

    def sent(w, carry):
        rz_copy(w).wait_send()
        return carry

    lax.fori_loop(0, z, sent, 0)

    def arrived(j, carry):
        slot = pl.ds(pl.multiple_of((z + j) * 16, 16), 16)
        remote(rz_out.at[pl.ds(0, 16), :], rz.at[slot, :], rz_sem, j, z_seq(z + j), sub).wait_recv()
        return carry

    lax.fori_loop(1, NZ - z, arrived, 0)
    term = own_term[...] + jnp.sum(rz[...].astype(F32).reshape(NZ, 16, FEAT), axis=0)
    last = iota((16, FEAT), 0) == 15
    for i in range(8):
        rows = slice(i * STRIDE + STRIDE - 16, (i + 1) * STRIDE)
        for acc, ref, lanes in ((dk_acc, dk_ref, slice(0, DH)), (dv_acc, dv_ref, slice(DH, FEAT))):
            extra = jnp.concatenate([term[i : i + 1, lanes], term[8 + i : 9 + i, lanes]], axis=1)
            ref[rows, :] = (acc[rows, :] + jnp.where(last, extra, 0.0)).astype(BF16)

    @pl.when(z == 0)
    def _():
        loss_pair(3).wait_send()
        loss_one(2, 2, 0).wait_recv()
        loss_one(3, 5, 0).wait_recv()

    @pl.when(z == 1)
    def _():
        loss_pair(2).wait_send()
        loss_one(2, 3, 1).wait_recv()
        loss_one(3, 6, 1).wait_recv()

    @pl.when(z == 2)
    def _():
        for copy in from2():
            copy.wait_send()
        loss_pair(2).wait_recv()
        loss_one(3, 7, 2).wait_recv()

    @pl.when(z == 3)
    def _():
        for copy in from3():
            copy.wait_send()
        loss_pair(3).wait_recv()
        loss_one(2, 4, 3).wait_recv()

    loss_ref[...] = jnp.sum(loss_z[...].reshape(NZ, 8, 128), axis=0)

    @pl.when(z < 2)
    def _():
        relay(3).wait_send()

    @pl.when(z == 2)
    def _():
        third().wait_send()


def emit(dq, dk, dv, loss, dq_out, dk_out, dv_out, loss_out, sems):
    copies = [
        pltpu.make_async_copy(src, dst, sems.at[i])
        for i, (src, dst) in enumerate([(dq, dq_out), (dk, dk_out), (dv, dv_out)])
    ]
    for copy in copies:
        copy.start()
    loss_out[...] = loss[0:1, 0:1]
    for copy in copies:
        copy.wait()


def local(queries, keys, values, offsets, negatives):
    vmem = pl.BlockSpec(memory_space=pltpu.VMEM)
    anywhere = pl.BlockSpec(memory_space=pl.ANY)
    wide = jax.ShapeDtypeStruct((ROWS, FEAT), BF16)

    def sems(count):
        return pltpu.SemaphoreType.DMA((2, count))

    outs = pl.pallas_call(
        kernel,
        out_shape=(wide, wide, wide, jax.ShapeDtypeStruct((8, 128), F32)),
        in_specs=[anywhere] * 5,
        out_specs=(vmem,) * 4,
        scratch_shapes=[
            pltpu.VMEM((WIDE, FEAT), BF16),
            pltpu.VMEM((ROWS, FEAT), BF16),
            pltpu.VMEM((ROWS, FEAT), BF16),
            pltpu.VMEM((4, 128), I32),
            pltpu.VMEM((15, ROWS), I32),
            pltpu.VMEM((OFFMAX, FEAT), BF16),
            pltpu.VMEM((OFFMAX, FEAT), BF16),
            pltpu.VMEM((NZ, NXY * 16, FEAT), BF16),
            pltpu.VMEM((PANEL, FEAT), BF16),
            pltpu.VMEM((PANEL, FEAT), BF16),
            pltpu.VMEM((FEAT, PANEL), BF16),
            pltpu.VMEM((FEAT, PANEL), BF16),
            pltpu.VMEM((FEAT, ROWS), BF16),
            pltpu.VMEM((FEAT, ROWS), BF16),
            pltpu.VMEM((PANEL, WIDE), F32),
            pltpu.VMEM((PANEL, ROWS), BF16),
            pltpu.VMEM((PANEL, WIDE), BF16),
            pltpu.VMEM((FEAT, WIDE), F32),
            pltpu.VMEM((WIDE, FEAT), BF16),
            pltpu.VMEM((FEAT, WIDE), BF16),
            pltpu.VMEM((ROWS, 128), I32),
            pltpu.VMEM((16, ROWS), I32),
            pltpu.VMEM((ROWS, 128), F32),
            pltpu.VMEM((NSUB * 16, ROWS), BF16),
            pltpu.VMEM((NSUB * 8, 128), F32),
            pltpu.VMEM((16, ROWS), F32),
            pltpu.VMEM((16, ROWS), F32),
            pltpu.VMEM((ROWS, ROWS), BF16),
            pltpu.VMEM((ROWS, ROWS), BF16),
            pltpu.VMEM((ROWS, 128), F32),
            pltpu.VMEM((FEAT, ROWS), F32),
            pltpu.VMEM((128, FEAT), BF16),
            pltpu.VMEM((128, FEAT), BF16),
            pltpu.VMEM((NXY * 8, 128), F32),
            pltpu.VMEM((NZ * 8, 128), F32),
            pltpu.VMEM((FEAT, ROWS), BF16),
            pltpu.VMEM((FEAT, ROWS), BF16),
            pltpu.VMEM((8, ROWS), F32),
            pltpu.VMEM((PANEL, FEAT), F32),
            pltpu.VMEM((PANEL, FEAT), F32),
            pltpu.VMEM((PANEL, ROWS), BF16),
            pltpu.VMEM((FEAT, ROWS), F32),
            pltpu.VMEM((NZ, NXY * 16, FEAT), BF16),
            pltpu.VMEM((NZ, NXY * 16, FEAT), BF16),
            pltpu.VMEM((NZ * 16, FEAT), BF16),
            pltpu.VMEM((NZ * 16, FEAT), BF16),
            pltpu.VMEM((16, FEAT), F32),
            pltpu.VMEM((ROWS, FEAT), F32),
            pltpu.VMEM((ROWS, FEAT), F32),
            pltpu.SemaphoreType.DMA((5,)),
            sems(3), sems(1), sems(1), sems(1), sems(4), sems(1), sems(1), sems(1), sems(8),
            sems(NZ - 1), sems(NXY), sems(NZ),
        ],
        compiler_params=pltpu.CompilerParams(
            collective_id=0, has_side_effects=True, vmem_limit_bytes=54400 * 1024
        ),
    )(queries, keys, values, offsets.reshape(4, 128), negatives.T)
    dq, dk, dv, loss = pl.pallas_call(
        emit,
        out_shape=(wide, wide, wide, jax.ShapeDtypeStruct((1, 1), F32)),
        in_specs=[anywhere] * 3 + [vmem],
        out_specs=(anywhere, anywhere, anywhere, vmem),
        scratch_shapes=[pltpu.SemaphoreType.DMA((3,))],
        compiler_params=pltpu.CompilerParams(vmem_limit_bytes=1024 * 1024),
    )(*outs)
    return dq, dk, dv, loss.reshape(())


def solution(mesh):
    placed = (P("seq", "sub"), P("seq", "sub"), P("seq", "sub"), P("seq"), P("seq", None))
    return jax.shard_map(
        local,
        mesh=mesh,
        in_specs=placed,
        out_specs=(P("seq", "sub"), P("seq", "sub"), P("seq", "sub"), P()),
        check_vma=False,
    )
```

```python
import math

import jax
import jax.numpy as jnp
from jax import lax
from jax.experimental import pallas as pl
from jax.experimental.pallas import tpu as pltpu
from jax.sharding import PartitionSpec as P

DH = 128
D = 2048
ROWS = 512
FEAT = 256
STRIDE = 64
OFFMAX = 64
NZ = 4
NXY = 16
NSUB = 8
NSEQ = 64
TOKENS = 32768
PANEL = 1024
WIDE = 640

EPSILON = 1e-05
TEMPER = 0.1
MASKED = -1e30
SCALE = 1.0 / math.sqrt(DH)
SCALE2 = SCALE * math.log2(math.e)

F32 = jnp.float32
BF16 = jnp.bfloat16
I32 = jnp.int32
MESH = pl.DeviceIdType.MESH


def nn(a, b):
    return lax.dot_general(a, b, (((1,), (0,)), ((), ())), preferred_element_type=F32)


def nt(a, b):
    return lax.dot_general(a, b, (((1,), (1,)), ((), ())), preferred_element_type=F32)


def tn(a, b):
    return lax.dot_general(a, b, (((0,), (0,)), ((), ())), preferred_element_type=F32)


def iota(shape, dim):
    return lax.broadcasted_iota(I32, shape, dim)


def pick_lanes(x, index):
    return jnp.take_along_axis(x, index, axis=1, mode="promise_in_bounds")


def split(x):
    high = x.astype(BF16)
    return high, (x - high.astype(F32)).astype(BF16)


def kernel(
    q_hbm, k_hbm, v_hbm, off_hbm,
    dq_ref, dk_ref, dv_ref, loss_ref,
    q, k, v, off, kx, vx, gat, kblk, vblk, kblk_t, vblk_t, k_t, v_t, s_scr, p1, p2, o1, att, att_t,
    idx, idx_t, picked, pk_buf, sq_buf, coef, rcoef, ct_hi, ct_lo, radial, grad_t,
    tail_out, tail_in, loss_xy, loss_z, out1, out2, delta, k_part, v_part, ds2, query2, gm, rs, rz_out, rz, own_term, dk_acc, dv_acc,
    load_sem, z_sem, own_sem, low_sem, mid_sem, near_sem, pk_sem, sq_sem, lxy_sem, lz_sem, rs_sem, plane_sem, rz_sem,
):
    seq = lax.axis_index("seq").astype(I32)
    sub = lax.axis_index("sub").astype(I32)
    z, xy = lax.div(seq, NXY), lax.rem(seq, NXY)
    nxt, prv = lax.rem(seq + 1, NSEQ), lax.rem(seq + NSEQ - 1, NSEQ)

    def z_seq(to):
        return to * NXY + xy

    def xy_peer(j):
        return z * NXY + lax.rem(xy + j, NXY)

    def sub_peer(j):
        return lax.rem(sub + j, NSUB)

    def remote(src, dst, sems, j, to_seq, to_sub):
        return pltpu.make_async_remote_copy(
            src_ref=src, dst_ref=dst, send_sem=sems.at[0, j], recv_sem=sems.at[1, j],
            device_id=(to_seq, to_sub), device_id_type=MESH,
        )

    def drain(ref, sems, i):
        whole = remote(ref, ref, sems, i, prv, sub)
        whole.wait_send()
        whole.wait_recv()

    def each(count, make, act):
        def body(j, carry):
            act(make(j))
            return carry

        lax.fori_loop(1, count, body, 0)

    def start(copy):
        copy.start()

    def finish(copy):
        copy.wait()

    loads = [
        pltpu.make_async_copy(src, dst, load_sem.at[i])
        for i, (src, dst) in enumerate(
            [(k_hbm, k), (v_hbm, v), (q_hbm, q.at[pl.ds(0, ROWS), :]), (off_hbm, off)]
        )
    ]
    for load in loads:
        load.start()

    gat[...] = jnp.zeros((NZ, NXY * 16, FEAT), BF16)
    rz[...] = jnp.zeros((NZ * 16, FEAT), BF16)
    rs[z] = jnp.zeros((NXY * 16, FEAT), BF16)
    tail_in[...] = jnp.zeros((128, FEAT), BF16)
    barrier = pltpu.get_barrier_semaphore()

    def greet(to_seq, to_sub):
        pl.semaphore_signal(barrier, inc=1, device_id=(to_seq, to_sub), device_id_type=MESH)

    greet(z_seq(lax.rem(z + 1, NZ)), sub)
    greet(z_seq(lax.rem(z + 3, NZ)), sub)

    @pl.when(z < 2)
    def _():
        greet(z_seq(z + 2), sub)

    each(NXY, xy_peer, lambda to: greet(to, sub))
    greet(nxt, sub)
    greet(prv, sub)
    each(NSUB, sub_peer, lambda to: greet(seq, to))

    own_row = pl.multiple_of(xy * 16, 16)
    own_rows = pl.ds(own_row, 16)
    chosen = (iota((16, ROWS), 1) == (iota((16, ROWS), 0) & 7) * STRIDE + (STRIDE - 1)).astype(F32).astype(BF16)
    first8 = iota((16, DH), 0) < 8
    loads[0].wait()
    loads[1].wait()
    k_sel = nn(chosen, k[...])
    v_sel = nn(chosen, v[...])
    gat[z, own_rows, :] = jnp.concatenate(
        [
            jnp.where(first8, k_sel[:, :DH], k_sel[:, DH:]),
            jnp.where(first8, v_sel[:, :DH], v_sel[:, DH:]),
        ],
        axis=1,
    ).astype(BF16)
    loads[2].wait()
    q[ROWS + OFFMAX :, :] = jnp.zeros((WIDE - ROWS - OFFMAX, FEAT), BF16)

    pl.semaphore_wait(barrier, 2 + (NXY - 1) + 2 + (NSUB - 1) + lax.div(z, 2))

    pair = gat.at[pl.ds(0, 2), own_rows, :]
    mine_tile = gat.at[z, own_rows, :]

    def swap():
        return remote(mine_tile, mine_tile, z_sem, 0, z_seq(1 - z), sub)

    def relay(to):
        return remote(pair, pair, z_sem, 1, z_seq(to), sub)

    def third():
        tile = gat.at[2, own_rows, :]
        return remote(tile, tile, z_sem, 2, z_seq(3), sub)

    def own_copy(j):
        return remote(mine_tile, mine_tile, own_sem, 0, xy_peer(j), sub)

    def low_copy(count):
        part = gat.at[pl.ds(0, count), own_rows, :]
        return lambda j: remote(part, part, low_sem, 0, xy_peer(j), sub)

    def mid_copy(j):
        part = gat.at[2, own_rows, :]
        return remote(part, part, mid_sem, 0, xy_peer(j), sub)

    @pl.when(z < 2)
    def _():
        swap().start()

    @pl.when(z == 2)
    def _():
        third().start()

    each(NXY, own_copy, start)
    near = [
        remote(q.at[pl.ds(0, OFFMAX), :], q.at[pl.ds(ROWS, OFFMAX), :], near_sem, 0, prv, sub),
        remote(k.at[pl.ds(0, OFFMAX), :], kx, near_sem, 1, prv, sub),
        remote(v.at[pl.ds(0, OFFMAX), :], vx, near_sem, 2, prv, sub),
    ]
    for copy in near:
        copy.start()

    @pl.when(z == 0)
    def _():
        swap().wait()
        relay(3).start()

    @pl.when(z == 1)
    def _():
        swap().wait()
        relay(2).start()
        each(NXY, low_copy(1), start)

    @pl.when(z == 2)
    def _():
        relay(2).wait_recv()
        each(NXY, low_copy(2), start)

    @pl.when(z == 3)
    def _():
        relay(3).wait_recv()
        each(NXY, low_copy(2), start)
        third().wait_recv()
        each(NXY, mid_copy, start)

    loads[3].wait()
    k_t[...] = k[...].T
    v_t[...] = v[...].T
    idx_t[0:15, :] = off[0:15, :]
    for b in range(4):
        cols = slice(b * 128, (b + 1) * 128)
        idx_t[15:16, cols] = off[15:16, cols] + iota((1, 128), 1) + b * 128
    for b in range(4):
        cols = slice(b * 128, (b + 1) * 128)
        idx[cols, :] = jnp.concatenate([idx_t[:, cols], jnp.zeros((112, 128), I32)], axis=0).T

    lane_q = iota((64, ROWS), 1)
    row_k = iota((64, ROWS), 0)

    def rows64(i, base=0):
        return pl.ds(pl.multiple_of(base + i * 64, 64), 64)

    m1, l1 = [], []
    for h in range(2):
        cols = slice(h * DH, (h + 1) * DH)
        base = h * ROWS
        s_scr[base : base + ROWS, 0:ROWS] = nt(k[:, cols], q[0:ROWS, cols])

        def top(i, best, base=base):
            x = s_scr[rows64(i, base), 0:ROWS]
            x = jnp.where(row_k + i * 64 <= lane_q, x, MASKED)
            s_scr[rows64(i, base), 0:ROWS] = x
            return jnp.maximum(best, jnp.max(x.reshape(8, 8, ROWS), axis=0))

        best = lax.fori_loop(0, 8, top, jnp.full((8, ROWS), MASKED, F32))
        level = jnp.max(best, axis=0, keepdims=True) * SCALE2

        def soft(i, total, base=base, level=level):
            p = jnp.exp2(s_scr[rows64(i, base), 0:ROWS] * SCALE2 - level)
            p1[rows64(i, base), :] = p.astype(BF16)
            return total + jnp.sum(p.reshape(8, 8, ROWS), axis=0)

        total = lax.fori_loop(0, 8, soft, jnp.zeros((8, ROWS), F32))
        m1.append(level)
        l1.append(jnp.sum(total, axis=0, keepdims=True))
        o1[cols, 0:ROWS] = nn(v_t[cols, :], p1[base : base + ROWS, :])
    for copy in near:
        copy.wait()
    for h in range(2):
        cols = slice(h * DH, (h + 1) * DH)
        x = nt(kx[:, cols], q[ROWS:WIDE, cols])
        x = jnp.where(iota((64, 128), 0) <= iota((64, 128), 1), x, MASKED)
        level = jnp.max(x, axis=0, keepdims=True) * SCALE2
        p = jnp.exp2(x * SCALE2 - level)
        m1[h] = jnp.concatenate([m1[h], level], axis=1)
        l1[h] = jnp.concatenate([l1[h], jnp.sum(p, axis=0, keepdims=True)], axis=1)
        o1[cols, ROWS:WIDE] = tn(vx[:, cols], p.astype(BF16))

    others = pl.ds(0, (NXY - 1) * 16)
    drain(gat.at[z, others, :], own_sem, 0)

    @pl.when(z == 1)
    def _():
        drain(gat.at[pl.ds(0, 1), others, :], low_sem, 0)

    @pl.when(z == 2)
    def _():
        drain(gat.at[pl.ds(0, 2), others, :], low_sem, 0)

    @pl.when(z == 3)
    def _():
        drain(gat.at[pl.ds(0, 2), others, :], low_sem, 0)

    in_first = (iota((256, DH), 0) & 15) < 8
    one = jnp.where(in_first, 1.0, 0.0).astype(BF16)
    two = jnp.where(in_first, 0.0, 1.0).astype(BF16)
    in_first_t = (iota((DH, 256), 1) & 15) < 8
    one_t = jnp.where(in_first_t, 1.0, 0.0).astype(BF16)
    two_t = jnp.where(in_first_t, 0.0, 1.0).astype(BF16)
    for b in (0, 1, 3, 2):
        if b == 2:

            @pl.when(z == 3)
            def _():
                drain(gat.at[2, others, :], mid_sem, 0)

        rows = slice(b * 256, (b + 1) * 256)
        for lanes, blk, blk_t in ((slice(0, DH), kblk, kblk_t), (slice(DH, FEAT), vblk, vblk_t)):
            tile = gat[b, :, lanes]
            tile_t = tile.T
            blk[rows, 0:DH] = tile * one
            blk[rows, DH:FEAT] = tile * two
            blk_t[0:DH, rows] = tile_t * one_t
            blk_t[DH:FEAT, rows] = tile_t * two_t
        s_scr[rows, :] = nt(kblk[rows, :], q[...])

    slab = lax.shift_right_logical(iota((64, WIDE), 0), 4)
    limit = jnp.where(iota((1, WIDE), 1) < ROWS, seq, nxt)

    def top2(i, best):
        x = s_scr[rows64(i), :]
        x = jnp.where(slab + i * 4 < limit, x, MASKED)
        s_scr[rows64(i), :] = x
        return jnp.maximum(best, jnp.max(x.reshape(4, 16, WIDE), axis=0))

    best = lax.fori_loop(0, NXY, top2, jnp.full((16, WIDE), MASKED, F32))
    m2 = [jnp.max(best[0:8], axis=0, keepdims=True) * SCALE2, jnp.max(best[8:16], axis=0, keepdims=True) * SCALE2]
    level16 = jnp.concatenate([jnp.broadcast_to(m2[0], (8, WIDE)), jnp.broadcast_to(m2[1], (8, WIDE))], axis=0)

    def soft2(i, total):
        p = jnp.exp2(s_scr[rows64(i), :].reshape(4, 16, WIDE) * SCALE2 - level16[None])
        p2[rows64(i), :] = p.reshape(64, WIDE).astype(BF16)
        return total + jnp.sum(p, axis=0)

    total = lax.fori_loop(0, NXY, soft2, jnp.zeros((16, WIDE), F32))
    l2 = [jnp.sum(total[0:8], axis=0, keepdims=True), jnp.sum(total[8:16], axis=0, keepdims=True)]
    o2 = nn(vblk_t[...], p2[...])
    w1, w2 = [], []
    squares = jnp.zeros((1, WIDE), F32)
    for h in range(2):
        cols = slice(h * DH, (h + 1) * DH)
        level = jnp.maximum(m1[h], m2[h])
        a1, a2 = jnp.exp2(m1[h] - level), jnp.exp2(m2[h] - level)
        inverse = 1.0 / (l1[h] * a1 + l2[h] * a2)
        a1, a2 = a1 * inverse, a2 * inverse
        w1.append(a1[:, 0:ROWS])
        w2.append(a2[:, 0:ROWS])
        out = (o1[cols, :] * a1 + o2[cols, :] * a2).astype(BF16)
        att_t[cols, :] = out
        wide = out.astype(F32)
        squares = squares + jnp.sum(wide * wide, axis=0, keepdims=True)

    sq_row = pl.multiple_of(sub * 8, 8)
    sq_buf[pl.ds(sq_row, 8), :] = jnp.concatenate(
        [squares[:, b * 128 : (b + 1) * 128] for b in range(5)] + [jnp.zeros((3, 128), F32)], axis=0
    )

    def sq_copy(j):
        part = sq_buf.at[pl.ds(sq_row, 8), :]
        return remote(part, part, sq_sem, 0, seq, sub_peer(j))

    each(NSUB, sq_copy, start)
    att[...] = att_t[...].T
    s_scr[0:ROWS, :] = nn(att[0:ROWS, :], att_t[...])

    def pick(i, carry):
        rows = rows64(i)
        here = idx[rows, :]
        low, high = here & 127, lax.shift_right_logical(here, 7)
        found = jnp.zeros((64, 128), F32)
        for b in range(5):
            value = pick_lanes(s_scr[rows, b * 128 : (b + 1) * 128], low)
            found = jnp.where(high == b, value, found)
        picked[rows, :] = found
        return carry

    lax.fori_loop(0, 8, pick, 0)
    pk_row = pl.multiple_of(sub * 16, 16)
    for b in range(4):
        lanes = slice(b * 128, (b + 1) * 128)
        pk_buf[pl.ds(pk_row, 16), lanes] = picked[lanes, :].T[0:16, :].astype(BF16)

    def pk_copy(j):
        part = pk_buf.at[pl.ds(pk_row, 16), :]
        return remote(part, part, pk_sem, 0, seq, sub_peer(j))

    each(NSUB, pk_copy, start)
    drain(sq_buf.at[pl.ds(0, (NSUB - 1) * 8), :], sq_sem, 0)
    radius = jnp.sqrt(jnp.sum(sq_buf[...].reshape(NSUB, 8, 128), axis=0) / D + EPSILON)
    own_radius = jnp.concatenate([radius[b : b + 1, :] for b in range(4)], axis=1)
    parts = []
    for c in range(4):
        here = idx_t[:, c * 128 : (c + 1) * 128]
        low, high = here & 127, lax.shift_right_logical(here, 7)
        found = jnp.ones((16, 128), F32)
        for b in range(5 if c == 3 else 4):
            value = pick_lanes(jnp.broadcast_to(radius[b : b + 1, :], (16, 128)), low)
            found = jnp.where(high == b, value, found)
        parts.append(found)
    pair_radius = jnp.concatenate(parts, axis=1)
    factor = 1.0 / (D * TEMPER * own_radius * pair_radius)
    pair_share = 1.0 / (D * pair_radius * pair_radius)
    own_share = 1.0 / (D * own_radius * own_radius)
    drain(pk_buf.at[pl.ds(0, (NSUB - 1) * 16), :], pk_sem, 0)
    dots = jnp.sum(pk_buf[...].astype(F32).reshape(NSUB, 16, ROWS), axis=0)

    logits = dots * factor
    powers = jnp.exp(logits)
    expsum = jnp.sum(powers, axis=0, keepdims=True)
    step = (seq * ROWS + iota((1, ROWS), 1)).astype(F32)
    weight = (1.0 + 2.0 * step / TOKENS) / TOKENS
    first = (iota((16, ROWS), 0) == 15).astype(F32)
    dlogits = (powers / expsum - first) * weight
    coef[...] = dlogits * factor
    pull = dlogits * logits
    rcoef[...] = pull * pair_share
    own_pull = jnp.sum(pull, axis=0, keepdims=True) * own_share

    late = slice(ROWS - 128, ROWS)
    ahead = att[ROWS:WIDE, :]
    late_mark = iota((128, 128), 0) + ROWS == idx_t[15:16, late]
    far_c = jnp.where(late_mark, coef[15:16, late], 0.0)
    far_r = jnp.sum(jnp.where(late_mark, rcoef[15:16, late], 0.0), axis=1, keepdims=True)
    far_hi, far_lo = split(far_c)
    tail = nn(far_hi, att[late, :]) + nn(far_lo, att[late, :]) - far_r * ahead.astype(F32)
    tail_out[...] = tail.astype(BF16)
    tail_copy = remote(tail_out.at[pl.ds(0, OFFMAX), :], tail_in.at[pl.ds(0, OFFMAX), :], near_sem, 3, nxt, sub)
    tail_copy.start()

    loss_part = jnp.sum(weight * (jnp.log(expsum) - logits[15:16, :]), axis=1, keepdims=True)
    lxy_row = pl.multiple_of(xy * 8, 8)
    loss_xy[pl.ds(lxy_row, 8), :] = jnp.broadcast_to(loss_part, (8, 128))

    def lxy_copy(j):
        part = loss_xy.at[pl.ds(lxy_row, 8), :]
        return remote(part, part, lxy_sem, 0, xy_peer(j), sub)

    each(NXY, lxy_copy, start)
    row_c = iota((16, ROWS), 0)

    def table(i, carry):
        rows = pl.ds(pl.multiple_of(i * 16, 16), 16)
        here = row_c + i * 16
        pairs = jnp.zeros((16, ROWS), F32)
        pulls = jnp.zeros((16, ROWS), F32)
        for k in range(16):
            same = here == idx_t[k : k + 1, :]
            pairs = pairs + jnp.where(same, coef[k : k + 1, :], 0.0)
            pulls = pulls + jnp.where(same, rcoef[k : k + 1, :], 0.0)
        ct_hi[rows, :], ct_lo[rows, :] = split(pairs)
        radial[rows, :] = pulls[:, 0:128] + pulls[:, 128:256] + pulls[:, 256:384] + pulls[:, 384:512]
        return carry

    lax.fori_loop(0, ROWS // 16, table, 0)
    rows_own = att[0:ROWS, :]
    radial_sum = jnp.sum(radial[...], axis=1, keepdims=True)
    cols_own = att_t[:, 0:ROWS]
    pushed = nn(ct_hi[...], rows_own) + nn(ct_lo[...], rows_own) - radial_sum * rows_own.astype(F32)
    grad_t[...] = nn(cols_own, ct_hi[...]) + nn(cols_own, ct_lo[...]) - own_pull * cols_own.astype(F32) + pushed.T
    grad_t[:, late] += tn(ahead, far_hi) + tn(ahead, far_lo)
    def scale(span):
        for h in range(2):
            cols = slice(h * DH, (h + 1) * DH)
            grad = grad_t[cols, span]
            wide = att_t[cols, span].astype(F32)
            one, two = (grad * w1[h][:, span]).astype(BF16), (grad * w2[h][:, span]).astype(BF16)
            out1[cols, span] = one
            out2[cols, span] = two
            delta[h : h + 1, span] = jnp.sum(one.astype(F32) * wide, axis=0, keepdims=True)
            delta[2 + h : 3 + h, span] = jnp.sum(two.astype(F32) * wide, axis=0, keepdims=True)

    def rows256(w):
        return pl.ds(pl.multiple_of(w * 256, 256), 256)

    def part(w, span, d16):
        rows = rows256(w)
        count = span.stop - span.start
        s_scr[0:256, span] = nn(vblk[rows, :], out2[:, span])

        def slope(i, carry):
            x = s_scr[rows64(i), span].reshape(4, 16, count) - d16[None]
            here = rows64(i, w * 256)
            p = p2[here, span].astype(F32).reshape(4, 16, count)
            ds2[here, span] = (x * p).reshape(64, count).astype(BF16)
            return carry

        lax.fori_loop(0, 4, slope, 0)
        return nn(ds2[rows, span], q[span, :]), nt(p2[rows, span], out2[:, span])

    def both_heads(span):
        count = span.stop - span.start
        return jnp.concatenate(
            [jnp.broadcast_to(delta[2:3, span], (8, count)), jnp.broadcast_to(delta[3:4, span], (8, count))], axis=0
        )

    most, few = slice(128, ROWS), slice(0, 128)
    scale(most)
    d_most = both_heads(most)

    def most_part(w, carry):
        rows = rows256(w)
        k_part[rows, :], v_part[rows, :] = part(w, most, d_most)
        return carry

    lax.fori_loop(0, z + 1, most_part, 0)
    tail_copy.wait()
    grad_t[:, few] += tail_in[...].astype(F32).T
    scale(few)
    d_few = both_heads(few)

    def rs_copy(w, sems, slot):
        def make(j):
            to = pl.ds(pl.multiple_of(lax.rem(xy + j, NXY) * 16, 16), 16)
            return remote(gm.at[w, to, :], rs.at[w, own_rows, :], sems, slot(j), xy_peer(j), sub)

        return make

    def wave(w, carry):
        rows = rows256(w)
        key2, value2 = part(w, few, d_few)
        key2 = key2 + k_part[rows, :]
        value2 = value2 + v_part[rows, :]
        head0 = (iota((256, DH), 0) & 15) < 8
        gm[w, :, 0:DH] = (jnp.where(head0, key2[:, :DH], key2[:, DH:]) * SCALE).astype(BF16)
        gm[w, :, DH:FEAT] = jnp.where(head0, value2[:, :DH], value2[:, DH:]).astype(BF16)

        rs[w, own_rows, :] = gm[w, own_rows, :]

        @pl.when(w < z)
        def _():
            each(NXY, rs_copy(w, rs_sem, lambda j: w), start)

        return carry

    lax.fori_loop(0, z + 1, wave, 0)

    plane_copy = rs_copy(z, plane_sem, lambda j: j)

    def send(j, carry):
        plane_copy(j).start()
        return carry

    lax.fori_loop(NXY - xy, NXY, send, 0)

    drain(loss_xy.at[pl.ds(0, (NXY - 1) * 8), :], lxy_sem, 0)
    plane_row = pl.ds(pl.multiple_of(z * 8, 8), 8)
    loss_z[plane_row, :] = jnp.sum(loss_xy[...].reshape(NXY, 8, 128), axis=0)

    def loss_swap():
        part = loss_z.at[plane_row, :]
        return remote(part, part, lz_sem, 0, z_seq(1 - z), sub)

    def loss_pair(to):
        part = loss_z.at[pl.ds(0, 16), :]
        return remote(part, part, lz_sem, 1, z_seq(to), sub)

    def loss_one(w, i, to):
        part = loss_z.at[pl.ds(w * 8, 8), :]
        return remote(part, part, lz_sem, i, z_seq(to), sub)

    def from2():
        return [loss_one(2, 2, 0), loss_one(2, 3, 1), loss_one(2, 4, 3)]

    def from3():
        return [loss_one(3, 5, 0), loss_one(3, 6, 1), loss_one(3, 7, 2)]

    @pl.when(z < 2)
    def _():
        loss_swap().start()

    @pl.when(z == 2)
    def _():
        for copy in from2():
            copy.start()

    @pl.when(z == 3)
    def _():
        for copy in from3():
            copy.start()

    query2[...] = jnp.zeros((FEAT, ROWS), F32)

    def far_query(w, carry):
        query2[...] += nn(kblk_t[:, rows256(w)], ds2[rows256(w), :])
        return carry

    lax.fori_loop(0, z + 1, far_query, 0)
    for h in range(2):
        cols = slice(h * DH, (h + 1) * DH)
        base = h * ROWS
        s_scr[base : base + ROWS, 0:ROWS] = nn(v[:, cols], out1[cols, :])

        def slope1(i, carry, base=base, h=h):
            x = s_scr[rows64(i, base), 0:ROWS] - delta[h : h + 1, :]
            s_scr[rows64(i, base), 0:ROWS] = x * p1[rows64(i, base), :].astype(F32)
            return carry

        lax.fori_loop(0, 8, slope1, 0)
        close = s_scr[base : base + ROWS, 0:ROWS].astype(BF16)
        query = (nn(k_t[cols, :], close) + query2[cols, :]) * SCALE
        dq_ref[:, cols] = query.T.astype(BF16)
        dk_acc[:, cols] = nn(close, q[0:ROWS, cols]) * SCALE
        dv_acc[:, cols] = nt(p1[base : base + ROWS, :], out1[cols, :])
    dk_ref[...] = dk_acc[...].astype(BF16)
    dv_ref[...] = dv_acc[...].astype(BF16)

    def plane_sum(w):
        return jnp.sum(rs[w].astype(F32).reshape(NXY, 16, FEAT), axis=0)

    rz_row = pl.multiple_of(z * 16, 16)

    def rz_copy(w):
        part = pl.ds(pl.multiple_of(w * 16, 16), 16)
        return remote(rz_out.at[part, :], rz.at[pl.ds(rz_row, 16), :], rz_sem, z - w, z_seq(w), sub)

    def down(w, carry):
        drain(rs.at[w, others, :], rs_sem, w)
        rz_out[pl.ds(pl.multiple_of(w * 16, 16), 16), :] = plane_sum(w).astype(BF16)
        rz_copy(w).start()
        return carry

    lax.fori_loop(0, z, down, 0)
    def plane_sent(j, carry):
        plane_copy(j).wait_send()
        return carry

    def plane_came(j, carry):
        plane_copy(j).wait_recv()
        return carry

    lax.fori_loop(xy + 1, NXY, plane_came, 0)
    lax.fori_loop(NXY - xy, NXY, plane_sent, 0)
    own_term[...] = plane_sum(z)

    @pl.when(z == 0)
    def _():
        loss_swap().wait()
        loss_pair(3).start()

    @pl.when(z == 1)
    def _():
        loss_swap().wait()
        loss_pair(2).start()

    def sent(w, carry):
        rz_copy(w).wait_send()
        return carry

    lax.fori_loop(0, z, sent, 0)

    def arrived(j, carry):
        slot = pl.ds(pl.multiple_of((z + j) * 16, 16), 16)
        remote(rz_out.at[pl.ds(0, 16), :], rz.at[slot, :], rz_sem, j, z_seq(z + j), sub).wait_recv()
        return carry

    lax.fori_loop(1, NZ - z, arrived, 0)
    term = own_term[...] + jnp.sum(rz[...].astype(F32).reshape(NZ, 16, FEAT), axis=0)
    last = iota((16, FEAT), 0) == 15
    for i in range(8):
        rows = slice(i * STRIDE + STRIDE - 16, (i + 1) * STRIDE)
        for acc, ref, lanes in ((dk_acc, dk_ref, slice(0, DH)), (dv_acc, dv_ref, slice(DH, FEAT))):
            extra = jnp.concatenate([term[i : i + 1, lanes], term[8 + i : 9 + i, lanes]], axis=1)
            ref[rows, :] = (acc[rows, :] + jnp.where(last, extra, 0.0)).astype(BF16)

    @pl.when(z == 0)
    def _():
        loss_pair(3).wait_send()
        loss_one(2, 2, 0).wait_recv()
        loss_one(3, 5, 0).wait_recv()

    @pl.when(z == 1)
    def _():
        loss_pair(2).wait_send()
        loss_one(2, 3, 1).wait_recv()
        loss_one(3, 6, 1).wait_recv()

    @pl.when(z == 2)
    def _():
        for copy in from2():
            copy.wait_send()
        loss_pair(2).wait_recv()
        loss_one(3, 7, 2).wait_recv()

    @pl.when(z == 3)
    def _():
        for copy in from3():
            copy.wait_send()
        loss_pair(3).wait_recv()
        loss_one(2, 4, 3).wait_recv()

    loss_ref[...] = jnp.sum(loss_z[...].reshape(NZ, 8, 128), axis=0)

    @pl.when(z < 2)
    def _():
        relay(3).wait_send()

    @pl.when(z == 2)
    def _():
        third().wait_send()


def emit(dq, dk, dv, loss, dq_out, dk_out, dv_out, loss_out, sems):
    copies = [
        pltpu.make_async_copy(src, dst, sems.at[i])
        for i, (src, dst) in enumerate([(dq, dq_out), (dk, dk_out), (dv, dv_out)])
    ]
    for copy in copies:
        copy.start()
    loss_out[...] = loss[0:1, 0:1]
    for copy in copies:
        copy.wait()


def local(queries, keys, values, offsets, negatives):
    vmem = pl.BlockSpec(memory_space=pltpu.VMEM)
    anywhere = pl.BlockSpec(memory_space=pl.ANY)
    wide = jax.ShapeDtypeStruct((ROWS, FEAT), BF16)

    def sems(count):
        return pltpu.SemaphoreType.DMA((2, count))

    outs = pl.pallas_call(
        kernel,
        out_shape=(wide, wide, wide, jax.ShapeDtypeStruct((8, 128), F32)),
        in_specs=[anywhere] * 4,
        out_specs=(vmem,) * 4,
        scratch_shapes=[
            pltpu.VMEM((WIDE, FEAT), BF16),
            pltpu.VMEM((ROWS, FEAT), BF16),
            pltpu.VMEM((ROWS, FEAT), BF16),
            pltpu.VMEM((16, ROWS), I32),
            pltpu.VMEM((OFFMAX, FEAT), BF16),
            pltpu.VMEM((OFFMAX, FEAT), BF16),
            pltpu.VMEM((NZ, NXY * 16, FEAT), BF16),
            pltpu.VMEM((PANEL, FEAT), BF16),
            pltpu.VMEM((PANEL, FEAT), BF16),
            pltpu.VMEM((FEAT, PANEL), BF16),
            pltpu.VMEM((FEAT, PANEL), BF16),
            pltpu.VMEM((FEAT, ROWS), BF16),
            pltpu.VMEM((FEAT, ROWS), BF16),
            pltpu.VMEM((PANEL, WIDE), F32),
            pltpu.VMEM((PANEL, ROWS), BF16),
            pltpu.VMEM((PANEL, WIDE), BF16),
            pltpu.VMEM((FEAT, WIDE), F32),
            pltpu.VMEM((WIDE, FEAT), BF16),
            pltpu.VMEM((FEAT, WIDE), BF16),
            pltpu.VMEM((ROWS, 128), I32),
            pltpu.VMEM((16, ROWS), I32),
            pltpu.VMEM((ROWS, 128), F32),
            pltpu.VMEM((NSUB * 16, ROWS), BF16),
            pltpu.VMEM((NSUB * 8, 128), F32),
            pltpu.VMEM((16, ROWS), F32),
            pltpu.VMEM((16, ROWS), F32),
            pltpu.VMEM((ROWS, ROWS), BF16),
            pltpu.VMEM((ROWS, ROWS), BF16),
            pltpu.VMEM((ROWS, 128), F32),
            pltpu.VMEM((FEAT, ROWS), F32),
            pltpu.VMEM((128, FEAT), BF16),
            pltpu.VMEM((128, FEAT), BF16),
            pltpu.VMEM((NXY * 8, 128), F32),
            pltpu.VMEM((NZ * 8, 128), F32),
            pltpu.VMEM((FEAT, ROWS), BF16),
            pltpu.VMEM((FEAT, ROWS), BF16),
            pltpu.VMEM((8, ROWS), F32),
            pltpu.VMEM((PANEL, FEAT), F32),
            pltpu.VMEM((PANEL, FEAT), F32),
            pltpu.VMEM((PANEL, ROWS), BF16),
            pltpu.VMEM((FEAT, ROWS), F32),
            pltpu.VMEM((NZ, NXY * 16, FEAT), BF16),
            pltpu.VMEM((NZ, NXY * 16, FEAT), BF16),
            pltpu.VMEM((NZ * 16, FEAT), BF16),
            pltpu.VMEM((NZ * 16, FEAT), BF16),
            pltpu.VMEM((16, FEAT), F32),
            pltpu.VMEM((ROWS, FEAT), F32),
            pltpu.VMEM((ROWS, FEAT), F32),
            pltpu.SemaphoreType.DMA((4,)),
            sems(3), sems(1), sems(1), sems(1), sems(4), sems(1), sems(1), sems(1), sems(8),
            sems(NZ - 1), sems(NXY), sems(NZ),
        ],
        compiler_params=pltpu.CompilerParams(
            collective_id=0, has_side_effects=True, vmem_limit_bytes=54400 * 1024
        ),
    )(queries, keys, values, jnp.concatenate([negatives.T, offsets[None, :]], axis=0))
    dq, dk, dv, loss = pl.pallas_call(
        emit,
        out_shape=(wide, wide, wide, jax.ShapeDtypeStruct((1, 1), F32)),
        in_specs=[anywhere] * 3 + [vmem],
        out_specs=(anywhere, anywhere, anywhere, vmem),
        scratch_shapes=[pltpu.SemaphoreType.DMA((3,))],
        compiler_params=pltpu.CompilerParams(vmem_limit_bytes=1024 * 1024),
    )(*outs)
    return dq, dk, dv, loss.reshape(())


def solution(mesh):
    placed = (P("seq", "sub"), P("seq", "sub"), P("seq", "sub"), P("seq"), P("seq", None))
    return jax.shard_map(
        local,
        mesh=mesh,
        in_specs=placed,
        out_specs=(P("seq", "sub"), P("seq", "sub"), P("seq", "sub"), P()),
        check_vma=False,
    )
```
